128 devices in a mesh: role: 4 (over x), ctx: 32 (over z, y, core).
Axes of the slice: x: 4, y: 4, z: 4, core: 2. Of those that a mesh axis runs over, the one named last changes fastest.
Arguments:
- prefill_hidden: bfloat16 [131072, 7168], P(('role', 'ctx')), may hold values from -6 to 6
- kv_down: bfloat16 [7168, 576], P('ctx'), may hold values from -0.0625 to 0.0625
- kv_gain: float32 [512], replicated, may hold values from 0.5 to 1.5
- q_nope: bfloat16 [8, 2, 128, 128], P('role', None, 'ctx'), may hold values from -8 to 8
- q_rope: bfloat16 [8, 2, 128, 64], P('role', None, 'ctx'), may hold values from -8 to 8
- key_up: bfloat16 [128, 128, 512], P('ctx'), may hold values from -0.5 to 0.5
- value_up: bfloat16 [128, 512, 128], P('ctx'), may hold values from -0.25 to 0.25
- latent_cache: bfloat16 [8, 32768, 576], P('role', 'ctx'), may hold values from -8 to 8
- cache_len: int32 [8], replicated, may hold values from 4096 to 32768
- page_list: int32 [32768, 1], replicated, may hold values from 0 to 255; in each aligned block of 256 rows (0 to 255, 256 to 511, ...) at most 2 rows name the same one
Outputs:
- attn_out: bfloat16 [8, 2, 128, 128], P('role', None, 'ctx')
The draws below stay inside these ranges and needn't reach their ends.
Inputs may be any that keep to these rules, and one draw needn't show every extreme that they name: `page_list`: aligned blocks of 256 pages are one device's pages; within one block no destination is named by more than 2 pages.
All inputs are finite; a program needn't handle non-finite values.
Results may differ from the reference program's by a relative error of at most 0.013.
Values may be sent and summed in bfloat16 or wider, within the bound.
A program may use at most 192 MiB of HBM per device.

```python
import math
import jax
import jax.numpy as jnp
import numpy as np
from jax import lax

D = 7168
LATENT = 512
ROPE = 64
HEADS = 128
NOPE = 128
VDIM = 128
PREF_DEV = 1024
PAGE = 4
REQ_GRP = 2
STEPS = 2
REQS = 8
CTX = 32768
PREF_ROWS = 131072
PAGES_DEV = 256
PAGES = 32768
BINS = 256
MOST = 2
N_CTX = 32
DEVICES = 128


def draw_q_rope(key, part):
    key = jax.random.fold_in(key, 11)
    values = jax.random.uniform(key, (REQS, STEPS, HEADS, ROPE), jnp.float32, -8.0, 8.0)
    return values.astype(jnp.bfloat16)


def draw_latent_cache(key, part):
    key = jax.random.fold_in(key, 13)
    key_value = jax.random.fold_in(key, 0)
    width = LATENT + ROPE
    values = jnp.clip(jax.random.normal(key_value, (REQS, CTX, width), jnp.float32), -6.0, 6.0)
    return values.astype(jnp.bfloat16)


def draw_cache_len(key, part):
    key = jax.random.fold_in(key, 17)
    key_len, key_top = jax.random.split(key)
    lengths = jax.random.randint(key_len, (REQS,), CTX // 8, CTX + 1)
    longest = jax.random.randint(key_top, (), 0, REQS)
    return jnp.where(jnp.arange(REQS) == longest, CTX, lengths).astype(jnp.int32)


def levels(rng, dims, cuts, low, largest):
    gain = 1.0
    for position, blocks in cuts:
        heights = jax.random.uniform(jax.random.fold_in(jax.random.fold_in(rng, 6), position), (blocks,), jnp.float32, low / len(cuts), largest / len(cuts))
        gain = gain * jnp.repeat(jnp.exp(heights), dims[position] // blocks).reshape((-1,) + (1,) * (len(dims) - 1 - position))
    return gain


def assign_block(key, own, number, rows, number_of, top, bound, skew):
    sequence = jax.random.permutation(key, number_of)
    heavy_load, usual = load_shares(number_of, rows * top, bound, skew, True), load_shares(number_of, rows * top, bound, skew, False)
    places = jnp.arange(number_of)

    def named(sizes, offset_by):
        used = int((sizes > 0).sum())
        fixed = max(1, used // 4)
        passed = fixed + (places - fixed + offset_by * (used - fixed)) % max(1, number_of - fixed)
        return jnp.zeros((number_of,), jnp.int32).at[sequence[jnp.where(places < fixed, places, passed)]].set(jnp.asarray(sizes, jnp.int32))

    sizes = jnp.where(number % 4 == 0, named(heavy_load, number // 4), named(usual, number - number // 4 - 1))
    mixed = jax.random.permutation(jax.random.fold_in(own, 3), number_of)
    source_of, receiver = mixed[0:number_of // 2 * 2:2], mixed[1:number_of // 2 * 2:2]
    room = jnp.minimum(sizes[source_of] - 1, bound - sizes[receiver]) // 2
    room = jnp.where((source_of == sequence[0]) | (receiver == sequence[0]) | (sizes[receiver] == 0), 0, jnp.maximum(room, 0))
    passed = jax.random.randint(jax.random.fold_in(own, 4), (number_of // 2,), 0, 1 << 20) % (room + 1)
    sizes = sizes.at[source_of].add(-passed).at[receiver].add(passed)
    labels = jnp.searchsorted(jnp.cumsum(sizes), jnp.arange(rows * top), side="right").astype(jnp.int32)
    listing = labels.reshape(top, rows).T
    listing = listing[jax.random.permutation(jax.random.fold_in(own, 1), rows)]
    offset_by = jax.random.randint(jax.random.fold_in(own, 2), (rows, 1), 0, top)
    return jnp.take_along_axis(listing, (jnp.arange(top)[None, :] + offset_by) % top, axis=1)


def load_shares(number_of, total, reach, skew, full):
    loads = [(1 << 20) // math.isqrt(standing ** skew) + 1 for standing in range(1, number_of + 1)]
    largest = reach if full else min(reach, max(-(-total // number_of), total * loads[0] // sum(loads)))
    least = 1 if total - largest >= number_of - 1 else 0
    counts, spare = [largest] + [least] * (number_of - 1), total - largest - least * (number_of - 1)
    while spare > 0:
        movable = [i for i in range(1, number_of) if counts[i] < largest] or [i for i in range(1, number_of) if counts[i] < reach]
        pool, remaining = sum([loads[i] for i in movable]), spare
        for i in movable:
            extra = min(reach - counts[i], max(1, remaining * loads[i] // pool), spare)
            counts[i] = counts[i] + extra
            spare = spare - extra
    return np.array(counts)


def noise(key, dims, scale, bound, pieces=(), held_as=jnp.bfloat16):
    loudness = levels(key, dims, pieces, -0.22, 0.18) if pieces else 1.0
    values = jax.random.normal(key, dims, jnp.float32) * scale * loudness
    return jnp.minimum(jnp.maximum(values, -bound), bound).astype(held_as)


def setup_inputs(seed: int = 0) -> dict:
    keys = jax.random.split(jax.random.key(seed), 11)
    prefill_hidden = noise(keys[0], (PREF_ROWS, D), 1.0, 6.0, ((0, 128),))
    kv_down = noise(keys[1], (D, LATENT + ROPE), D ** -0.5, 0.0625, ((0, 32),))
    kv_gain = jnp.clip(1.0 + 0.1 * jax.random.normal(keys[2], (LATENT,), jnp.float32), 0.5, 1.5)
    q_nope = noise(keys[3], (REQS, STEPS, HEADS, NOPE), 1.5, 8.0, ((0, 4), (2, 32)))
    q_rope = draw_q_rope(jax.random.fold_in(keys[10], 71), 0)
    key_up = noise(keys[5], (HEADS, NOPE, LATENT), NOPE ** -0.5, 0.5, ((0, 32),))
    value_up = noise(keys[6], (HEADS, LATENT, VDIM), LATENT ** -0.5, 0.25, ((0, 32),))
    latent_cache = draw_latent_cache(jax.random.fold_in(keys[10], 71), 0)
    cache_len = draw_cache_len(jax.random.fold_in(keys[10], 71), 0)
    page_list_keys = jax.random.split(jax.random.fold_in(keys[9], 1), PAGES // PAGES_DEV)
    page_list_turns = jax.random.permutation(jax.random.fold_in(keys[9], 3), PAGES // PAGES_DEV)
    page_list = jax.vmap(lambda own, number: assign_block(jax.random.fold_in(keys[9], 2), own, number, PAGES_DEV, BINS, 1, MOST, 2))(page_list_keys, page_list_turns).reshape((PAGES, 1))
    return {"prefill_hidden": prefill_hidden, "kv_down": kv_down, "kv_gain": kv_gain, "q_nope": q_nope, "q_rope": q_rope, "key_up": key_up, "value_up": value_up, "latent_cache": latent_cache, "cache_len": cache_len, "page_list": page_list}


def compress(hidden_rows, kv_down, kv_gain):
    projected = jnp.dot(hidden_rows, kv_down, preferred_element_type=jnp.float32)
    latent_part = projected[:, :LATENT]
    inverse = lax.rsqrt(lax.optimization_barrier(jnp.mean(latent_part * latent_part, axis=-1, keepdims=True)) + 1e-06)
    return jnp.concatenate([latent_part * inverse * kv_gain, projected[:, LATENT:]], axis=-1).astype(jnp.bfloat16)

def reference(prefill_hidden, kv_down, kv_gain, q_nope, q_rope, key_up, value_up, latent_cache, cache_len, page_list):
    width = LATENT + ROPE
    blocks = prefill_hidden.reshape(DEVICES, PREF_DEV, D)
    new_rows = lax.map(lambda block: compress(block, kv_down, kv_gain), blocks).reshape(DEVICES * PREF_DEV, width)
    absorbed = jnp.einsum('rthn,hnc->rthc', q_nope.astype(jnp.float32), key_up.astype(jnp.float32)).astype(jnp.bfloat16)
    query = jnp.concatenate([absorbed, q_rope], axis=-1)
    bins = page_list[:, 0]
    page_request = bins // (REQ_GRP * N_CTX) * REQ_GRP + bins % REQ_GRP
    row_request = jnp.repeat(page_request, PAGE)
    scale = 1.0 / math.sqrt(NOPE + ROPE)
    low = jnp.float32(-1e+30)

    def one_request(request):
        queries = query[request].reshape(STEPS * HEADS, width)
        cache_rows = latent_cache[request]
        score_old = jnp.dot(queries, cache_rows.T, preferred_element_type=jnp.float32) * scale
        score_new = jnp.dot(queries, new_rows.T, preferred_element_type=jnp.float32) * scale
        live_old = (jnp.arange(CTX, dtype=jnp.int32) < cache_len[request])[None, :]
        live_new = (row_request == request)[None, :]
        best = jnp.maximum(lax.optimization_barrier(jnp.max(jnp.where(live_old, score_old, low), axis=1)), lax.optimization_barrier(jnp.max(jnp.where(live_new, score_new, low), axis=1)))
        weight_old = jnp.where(live_old, jnp.exp(score_old - best[:, None]), 0.0)
        weight_new = jnp.where(live_new, jnp.exp(score_new - best[:, None]), 0.0)
        total = lax.optimization_barrier(jnp.sum(weight_old, axis=1)) + lax.optimization_barrier(jnp.sum(weight_new, axis=1))
        summed = jnp.dot(weight_old.astype(jnp.bfloat16), cache_rows[:, :LATENT], preferred_element_type=jnp.float32)
        summed = summed + jnp.dot(weight_new.astype(jnp.bfloat16), new_rows[:, :LATENT], preferred_element_type=jnp.float32)
        return (summed / total[:, None]).astype(jnp.bfloat16).reshape(STEPS, HEADS, LATENT)
    latent_out = lax.map(one_request, jnp.arange(REQS, dtype=jnp.int32))
    return jnp.einsum('rthc,hcv->rthv', latent_out.astype(jnp.float32), value_up.astype(jnp.float32)).astype(jnp.bfloat16)
```

```python
import functools
import math

import jax
import jax.numpy as jnp
from jax import lax
from jax.experimental import pallas as pl
from jax.experimental.pallas import tpu as pltpu
from jax.sharding import PartitionSpec as P

LATENT = 512
PAGE = 4
LOW = -1e30
FLOOR = -1e29
TAIL = 640


def place():
    role = lax.axis_index("role")
    ctx = lax.axis_index("ctx")
    return role, ctx // 8, (ctx // 2) % 4, ctx % 2


def ctx_of(z, y, core):
    return (z * 4 + y) * 2 + core


def gather_kernel(
    hidden_hbm,
    kv_hbm,
    gain_ref,
    query_ref,
    rows_ref,
    queries_ref,
    hidden,
    weights,
    total,
    load_sem,
    kv_send,
    kv_recv,
    pair_send,
    pair_recv,
    q_send,
    q_recv,
    q_pair_send,
    q_pair_recv,
):
    x, z, y, core = place()
    depth = kv_hbm.shape[0]
    half = depth // 2
    chunk = depth * 8

    barrier = pltpu.get_barrier_semaphore()
    others = [{"ctx": ctx_of(z, y, 1 - core)}]
    for step in (1, 2, 3):
        others.append({"ctx": ctx_of((z + step) % 4, y, core)})
        others.append({"ctx": ctx_of(z, (y + step) % 4, core)})
        others.append({"role": (x + step) % 4})
    for other in others:
        pl.semaphore_signal(barrier, inc=1, device_id=other, device_id_type=pl.DeviceIdType.MESH)

    line = [z, (z + 3) % 4, (z + 1) % 4, (z + 2) % 4]
    loads = []
    for index in range(4):
        columns = pl.ds(pl.multiple_of(line[index] * chunk, 128), chunk)
        load = pltpu.make_async_copy(
            hidden_hbm.at[:, columns], hidden.at[:, columns], load_sem.at[index]
        )
        loads.append(load)
    own_rows = pl.ds(pl.multiple_of(ctx_of(z, y, core) * depth, 16), depth)
    own_load = pltpu.make_async_copy(kv_hbm, weights.at[own_rows, :], load_sem.at[4])
    own_load.start()
    queries_ref[x, z, y, core] = query_ref[...]
    own_load.wait()
    loads[0].start()
    pl.semaphore_wait(barrier, len(others))

    def piece(z_at, y_at, core_at, part):
        start = ctx_of(z_at, y_at, core_at) * depth + part * half
        return weights.at[pl.ds(pl.multiple_of(start, 16), half), :]

    def spot(part, first, second):
        return (second, first) if part == 0 else (first, second)

    mine = [(y, z), (z, y)]
    sends = []

    def send(part, slot, where, target):
        ref = piece(*spot(part, *where), core, part)
        copy = pltpu.make_async_remote_copy(
            src_ref=ref,
            dst_ref=ref,
            send_sem=kv_send.at[part, slot],
            recv_sem=kv_recv.at[part, slot],
            device_id={"ctx": ctx_of(*spot(part, *target), core)},
            device_id_type=pl.DeviceIdType.MESH,
        )
        copy.start()
        sends.append(copy)

    def pair(part, slot, where, core_at):
        ref = piece(*spot(part, *where), core_at, part)
        return pltpu.make_async_remote_copy(
            src_ref=ref,
            dst_ref=ref,
            send_sem=pair_send.at[part, slot],
            recv_sem=pair_recv.at[part, slot],
            device_id={"ctx": ctx_of(z, y, 1 - core)},
            device_id_type=pl.DeviceIdType.MESH,
        )

    def wait_recv(part, slot, where):
        ref = piece(*spot(part, *where), core, part)
        pltpu.make_async_remote_copy(
            src_ref=ref,
            dst_ref=ref,
            send_sem=kv_send.at[part, slot],
            recv_sem=kv_recv.at[part, slot],
            device_id={"ctx": ctx_of(z, y, 1 - core)},
            device_id_type=pl.DeviceIdType.MESH,
        ).wait_recv()

    def places(part):
        first, second = mine[part]
        along = [first, (first + 3) % 4, (first + 1) % 4, (first + 2) % 4]
        found = {15: (first, second), 0: (along[1], second), 1: (along[2], second), 2: (along[3], second)}
        for index in range(4):
            found[3 + index] = (along[index], (second + 3) % 4)
            found[7 + index] = (along[index], (second + 1) % 4)
            found[11 + index] = (along[index], (second + 2) % 4)
        return found

    table = [places(0), places(1)]

    def pass_on(part, slot):
        copy = pair(part, slot, table[part][slot], core)
        copy.start()
        sends.append(copy)

    def spread(part, index):
        first, second = mine[part]
        where = table[part][(15, 0, 1, 2)[index]]
        send(part, 3 + index, where, (first, (second + 1) % 4))
        send(part, 7 + index, where, (first, (second + 3) % 4))

    def event(part, slot):
        first, second = mine[part]
        where = table[part][slot]
        wait_recv(part, slot, where)
        if slot == 1:
            turn = 1 - 2 * core
            send(part, 2, ((first - turn + 4) % 4, second), ((first + turn + 4) % 4, second))
        if 11 > slot >= 3:
            index = (slot - 3) % 4
            if slot < 7 and index in (0, 3):
                send(part, 11 + index, where, (first, (second + 1) % 4))
            if slot >= 7 and index in (1, 2):
                send(part, 11 + index, where, (first, (second + 3) % 4))
        if slot < 3:
            spread(part, slot + 1)
        pass_on(part, slot)

    q_sends = []

    def q_block(stage, z_at, y_at, x_at):
        if stage == 0:
            return queries_ref.at[x, z_at, y, core]
        if stage == 1:
            return queries_ref.at[x, :, y_at, core]
        return queries_ref.at[x_at, :, :, core]

    def q_copy(stage, step, sending):
        sign = 0 if sending else 4 - step
        at = [(v + sign) % 4 for v in (z, y, x)]
        ref = q_block(stage, *at)
        target = [
            {"ctx": ctx_of((z + step) % 4, y, core)},
            {"ctx": ctx_of(z, (y + step) % 4, core)},
            {"role": (x + step) % 4},
        ][stage]
        return pltpu.make_async_remote_copy(
            src_ref=ref,
            dst_ref=ref,
            send_sem=q_send.at[stage, step],
            recv_sem=q_recv.at[stage, step],
            device_id=target,
            device_id_type=pl.DeviceIdType.MESH,
        )

    def q_start(stage):
        for step in (1, 3, 2):
            copy = q_copy(stage, step, True)
            copy.start()
            q_sends.append(copy)

    def q_wait(stage):
        for step in (1, 3, 2):
            q_copy(stage, step, False).wait_recv()

    def q_pair(step, core_at):
        ref = queries_ref.at[(x + step) % 4, :, :, core_at]
        return pltpu.make_async_remote_copy(
            src_ref=ref,
            dst_ref=ref,
            send_sem=q_pair_send.at[step],
            recv_sem=q_pair_recv.at[step],
            device_id={"ctx": ctx_of(z, y, 1 - core)},
            device_id_type=pl.DeviceIdType.MESH,
        )

    def q_pass(step):
        copy = q_pair(step, core)
        copy.start()
        q_sends.append(copy)

    def multiply(index, tile):
        if tile == 0:
            slots = [
                (0, (15, 0, 1, 2)),
                (0, (3, 4, 5, 6)),
                (0, (7, 8, 9, 10)),
                (0, (11, 12, 13, 14)),
            ][index], (1, ((15, 0, 1, 2)[index], 3 + index, 7 + index, 11 + index))
            for part, group in slots:
                for slot in group:
                    pair(part, slot, table[part][slot], 1 - core).wait_recv()
            loads[index].wait()
        columns = pl.ds(pl.multiple_of(line[index] * chunk, 128), chunk)
        down = pl.ds(pl.multiple_of(line[index] * chunk, 16), chunk)
        span = pl.ds(tile * 256, 256)
        product = jnp.dot(
            hidden[span, columns], weights[down, :], preferred_element_type=jnp.float32
        )
        if index == 0:
            total[span, :] = product
        else:
            total[span, :] += product

    for part in (0, 1):
        first, second = mine[part]
        send(part, 0, (first, second), ((first + 1) % 4, second))
        send(part, 1, (first, second), ((first + 3) % 4, second))
    q_start(0)
    for part in (0, 1):
        pass_on(part, 15)
        spread(part, 0)
    for load in loads[1:]:
        load.start()
    for slot in (0, 1):
        for part in (0, 1):
            event(part, slot)
    q_wait(0)
    q_start(1)
    for slot in (3, 7, 2):
        for part in (0, 1):
            event(part, slot)
    q_wait(1)
    q_start(2)
    q_pass(0)
    plan = [
        (11,), (4,), (0, 0), (8,), (0, 1), (5,), (0, 2), (9,), (0, 3), (6,), (10,), (12,), (1, 0), (13,), (1, 1), (14,),
        (1, 2), (1, 3), (2, 0), (2, 1), (2, 2), (2, 3), (3, 0), (3, 1), (3, 2), (3, 3),
    ]
    for entry in plan:
        if len(entry) == 1:
            for part in (0, 1):
                event(part, entry[0])
        else:
            multiply(*entry)
    q_wait(2)
    for step in (1, 2, 3):
        q_pass(step)

    for tile in range(4):
        span = pl.ds(tile * 256, 256)
        latent = total[span, :LATENT]
        inverse = lax.rsqrt(jnp.mean(latent * latent, axis=-1, keepdims=True) + 1e-06)
        rows_ref[span, :LATENT] = (latent * inverse * gain_ref[...]).astype(jnp.bfloat16)
        rows_ref[span, LATENT:] = total[span, LATENT:].astype(jnp.bfloat16)

    for step in range(4):
        q_pair(step, 1 - core).wait_recv()
    for copy in sends + q_sends:
        copy.wait_send()


def compress(prefill_hidden, kv_down, kv_gain, query_part):
    rows, width = prefill_hidden.shape[0], kv_down.shape[1]
    vmem = pl.BlockSpec(memory_space=pltpu.VMEM)
    hbm = pl.BlockSpec(memory_space=pl.ANY)
    return pl.pallas_call(
        gather_kernel,
        out_shape=(
            jax.ShapeDtypeStruct((rows, width), jnp.bfloat16),
            jax.ShapeDtypeStruct((4, 4, 4, 2) + query_part.shape, jnp.bfloat16),
        ),
        in_specs=[hbm, hbm, vmem, vmem],
        out_specs=(vmem, vmem),
        scratch_shapes=[
            pltpu.VMEM(prefill_hidden.shape, jnp.bfloat16),
            pltpu.VMEM((prefill_hidden.shape[1], width), jnp.bfloat16),
            pltpu.VMEM((rows, width), jnp.float32),
            pltpu.SemaphoreType.DMA((5,)),
            pltpu.SemaphoreType.DMA((2, 15)),
            pltpu.SemaphoreType.DMA((2, 15)),
            pltpu.SemaphoreType.DMA((2, 16)),
            pltpu.SemaphoreType.DMA((2, 16)),
            pltpu.SemaphoreType.DMA((3, 4)),
            pltpu.SemaphoreType.DMA((3, 4)),
            pltpu.SemaphoreType.DMA((4,)),
            pltpu.SemaphoreType.DMA((4,)),
        ],
        compiler_params=pltpu.CompilerParams(
            collective_id=0, has_side_effects=True, vmem_limit_bytes=60 * 2**20
        ),
    )(prefill_hidden, kv_down, kv_gain.reshape(1, -1), query_part)


def chip_device(chip, core):
    return {"role": chip // 16, "ctx": (chip % 16) * 2 + core}


def join_kernel(
    scale,
    queries_ref,
    rows_ref,
    cache_ref,
    owner_ref,
    length_ref,
    up_ref,
    out_ref,
    partial,
    pair_in,
    outgoing,
    arrived,
    pair_send,
    pair_recv,
    send_sem,
    recv_sem,
    local_sem,
):
    x, z, y, core = place()
    chip = x * 16 + z * 4 + y
    barrier = pltpu.get_barrier_semaphore()

    @pl.loop(1, 64)
    def _(step):
        pl.semaphore_signal(
            barrier,
            inc=1,
            device_id=chip_device((chip + step) % 64, core),
            device_id_type=pl.DeviceIdType.MESH,
        )

    sibling = {"ctx": ctx_of(z, y, 1 - core)}
    pl.semaphore_signal(barrier, inc=1, device_id=sibling, device_id_type=pl.DeviceIdType.MESH)

    def queries_of(group, request):
        block = queries_ref[group].reshape(32, 16, 576).astype(jnp.float32)
        return block[:, request * 8 : request * 8 + 8].reshape(256, 576).astype(jnp.bfloat16)

    def attend(queries, keys, live):
        scores = lax.dot_general(
            queries, keys, (((1,), (1,)), ((), ())), preferred_element_type=jnp.float32
        )
        scores = jnp.where(live, scores * scale, LOW)
        best = jnp.maximum(jnp.max(scores, axis=1, keepdims=True), FLOOR)
        weight = jnp.exp2(scores - best)
        amount = jnp.sum(weight, axis=1, keepdims=True)
        summed = jnp.dot(
            weight.astype(jnp.bfloat16), keys[:, :LATENT], preferred_element_type=jnp.float32
        )
        return best, amount, summed

    def pack(block, mark):
        head = mark.astype(jnp.bfloat16).astype(jnp.float32)
        rest = mark - head
        middle = rest.astype(jnp.bfloat16).astype(jnp.float32)
        last = rest - middle
        lane = lax.broadcasted_iota(jnp.int32, mark.shape[:-1] + (TAIL - LATENT,), mark.ndim - 1)
        tail = jnp.where(lane == 0, head, jnp.where(lane == 1, middle, jnp.where(lane == 2, last, 0.0)))
        return block.astype(jnp.bfloat16), tail.astype(jnp.bfloat16)

    def mark_of(tail):
        return jnp.sum(tail.astype(jnp.float32), axis=-1, keepdims=True)

    def compute(step, group, with_cache):
        blocks, marks = [], []
        for request in (0, 1):
            queries = queries_of(group, request)
            live = owner_ref[...] == group * 2 + request
            best, amount, summed = attend(queries, rows_ref[...], live)
            if with_cache:
                keys = cache_ref[request]
                slots = keys.shape[0]
                first = ctx_of(z, y, core) * slots
                position = first + lax.broadcasted_iota(jnp.int32, (1, slots), 1)
                old_best, old_amount, old_summed = attend(
                    queries, keys, position < length_ref[request]
                )
                new_best = jnp.maximum(best, old_best)
                factor, old_factor = jnp.exp2(best - new_best), jnp.exp2(old_best - new_best)
                amount = amount * factor + old_amount * old_factor
                summed = summed * factor + old_summed * old_factor
                best = new_best
            some = amount > 0.0
            amount = jnp.where(some, amount, 1.0)
            mark = jnp.where(some, best + jnp.log2(amount), LOW)
            blocks.append((summed / amount).reshape(32, 8, LATENT))
            marks.append(mark.reshape(32, 8, 1))
        block, tail = pack(jnp.concatenate(blocks, axis=1), jnp.concatenate(marks, axis=1))
        partial[step, :, :, :, :LATENT] = block.reshape(16, 2, 16, LATENT)
        partial[step, :, :, :, LATENT:] = tail.reshape(16, 2, 16, TAIL - LATENT)

    def pair_copy(step):
        return pltpu.make_async_remote_copy(
            src_ref=partial.at[step, :, 1 - core],
            dst_ref=pair_in.at[step],
            send_sem=pair_send.at[step],
            recv_sem=pair_recv.at[step],
            device_id=sibling,
            device_id_type=pl.DeviceIdType.MESH,
        )

    def message(step, group, turn):
        spot = (z * 4 + y + turn) % 16
        return pltpu.make_async_remote_copy(
            src_ref=outgoing.at[step, spot],
            dst_ref=arrived.at[chip],
            send_sem=send_sem.at[step, turn],
            recv_sem=recv_sem.at[chip],
            device_id=chip_device(group * 16 + spot, core),
            device_id_type=pl.DeviceIdType.MESH,
        )

    def finish(step, group, first_turn):
        pair_copy(step).wait_recv()
        one = partial.at[step, :, core]
        two = pair_in.at[step]
        one_mark, two_mark = mark_of(one[:, :, LATENT:]), mark_of(two[:, :, LATENT:])
        best = jnp.maximum(one_mark, two_mark)
        one_weight, two_weight = jnp.exp2(one_mark - best), jnp.exp2(two_mark - best)
        amount = one_weight + two_weight
        block = one[:, :, :LATENT].astype(jnp.float32) * (one_weight / amount) + two[
            :, :, :LATENT
        ].astype(jnp.float32) * (two_weight / amount)
        block, tail = pack(block, jnp.maximum(best + jnp.log2(amount), LOW))
        outgoing[step, :, :, :LATENT] = block
        outgoing[step, :, :, LATENT:] = tail

        @pl.loop(first_turn, 16)
        def _(turn):
            message(step, group, turn).start()

    for step in range(4):
        group = (x + 1 + step) % 4
        compute(step, group, step == 3)
        if step == 0:
            pl.semaphore_wait(barrier, 64)
        pair_copy(step).start()
        if step > 0:
            finish(step - 1, (x + step) % 4, 0)
    finish(3, x, 1)
    own = pltpu.make_async_copy(outgoing.at[3, z * 4 + y], arrived.at[chip], local_sem)
    own.start()
    own.wait()

    @pl.loop(1, 64)
    def _(step):
        source = (chip + step) % 64
        pltpu.make_async_remote_copy(
            src_ref=arrived.at[source],
            dst_ref=arrived.at[source],
            send_sem=send_sem.at[0, 0],
            recv_sem=recv_sem.at[source],
            device_id=sibling,
            device_id_type=pl.DeviceIdType.MESH,
        ).wait_recv()

    marks = mark_of(arrived[:, :, LATENT:])
    best = jnp.max(marks, axis=0, keepdims=True)
    weight = jnp.exp2(marks - best)
    amount = jnp.sum(weight, axis=0)
    summed = jnp.sum(arrived[:, :, :LATENT].astype(jnp.float32) * weight, axis=0)
    latent = (summed / amount).astype(jnp.bfloat16)
    heads = up_ref.shape[0]
    row = lax.broadcasted_iota(jnp.int32, (16, 1), 0) % heads
    result = jnp.zeros(out_ref.shape, jnp.float32)
    for head in range(heads):
        product = jnp.dot(latent, up_ref[head], preferred_element_type=jnp.float32)
        result = jnp.where(row == head, product, result)
    out_ref[...] = result.astype(jnp.bfloat16)

    for step in range(4):
        pair_copy(step).wait_send()

        @pl.loop(1 if step == 3 else 0, 16)
        def _(turn):
            message(step, (x + 1 + step) % 4, turn).wait_send()


def join(queries, rows, cache, owner, lengths, value_up, scale):
    vmem = pl.BlockSpec(memory_space=pltpu.VMEM)
    smem = pl.BlockSpec(memory_space=pltpu.SMEM)
    return pl.pallas_call(
        functools.partial(join_kernel, scale),
        out_shape=jax.ShapeDtypeStruct((16, value_up.shape[2]), jnp.bfloat16),
        in_specs=[vmem, vmem, vmem, vmem, smem, vmem],
        out_specs=vmem,
        scratch_shapes=[
            pltpu.VMEM((4, 16, 2, 16, TAIL), jnp.bfloat16),
            pltpu.VMEM((4, 16, 16, TAIL), jnp.bfloat16),
            pltpu.VMEM((4, 16, 16, TAIL), jnp.bfloat16),
            pltpu.VMEM((64, 16, TAIL), jnp.bfloat16),
            pltpu.SemaphoreType.DMA((4,)),
            pltpu.SemaphoreType.DMA((4,)),
            pltpu.SemaphoreType.DMA((4, 16)),
            pltpu.SemaphoreType.DMA((64,)),
            pltpu.SemaphoreType.DMA,
        ],
        compiler_params=pltpu.CompilerParams(
            collective_id=1, has_side_effects=True, vmem_limit_bytes=60 * 2**20
        ),
    )(queries, rows, cache, owner, lengths, value_up)


def local(
    prefill_hidden,
    kv_down,
    kv_gain,
    q_nope,
    q_rope,
    key_up,
    value_up,
    latent_cache,
    cache_len,
    page_list,
):
    count_ctx = lax.axis_size("ctx")
    role_index = lax.axis_index("role")
    my_device = role_index * count_ctx + lax.axis_index("ctx")
    req_grp = q_nope.shape[0]
    pages_dev = prefill_hidden.shape[0] // PAGE
    scale = math.log2(math.e) / math.sqrt(q_nope.shape[3] + q_rope.shape[3])
    absorbed = jnp.einsum(
        "rthn,hnc->rthc", q_nope, key_up, preferred_element_type=jnp.float32
    ).astype(jnp.bfloat16)
    query_part = jnp.concatenate([absorbed, q_rope], axis=-1)
    query_part = query_part.reshape(-1, query_part.shape[-1])
    rows, queries = compress(prefill_hidden, kv_down, kv_gain, query_part)
    bins = lax.dynamic_slice_in_dim(page_list[:, 0], my_device * pages_dev, pages_dev)
    request = bins // (req_grp * count_ctx) * req_grp + bins % req_grp
    owner = jnp.repeat(request, PAGE)[None, :]
    lengths = lax.dynamic_slice_in_dim(cache_len, role_index * req_grp, req_grp)
    out = join(queries, rows, latent_cache, owner, lengths, value_up, scale)
    return out.reshape(q_nope.shape[:3] + (value_up.shape[2],))


def solution(mesh):
    return jax.shard_map(
        local,
        mesh=mesh,
        in_specs=(
            P(("role", "ctx"), None),
            P("ctx", None),
            P(),
            P("role", None, "ctx", None),
            P("role", None, "ctx", None),
            P("ctx", None, None),
            P("ctx", None, None),
            P("role", "ctx", None),
            P(),
            P(),
        ),
        out_specs=P("role", None, "ctx", None),
        check_vma=False,
    )
```

```python
import functools
import math

import jax
import jax.numpy as jnp
from jax import lax
from jax.experimental import pallas as pl
from jax.experimental.pallas import tpu as pltpu
from jax.sharding import PartitionSpec as P

LATENT = 512
PAGE = 4
LOW = -1e30
FLOOR = -1e29
TAIL = 640
MESH = pl.DeviceIdType.MESH
TURNS = (2, 1, 3, 0)
ONWARD = (0, 1)
PLAN = (
    ("q", 0), ("q", 1), ("p", 0, 0), ("p", 1, 0), ("p", 0, 1), ("p", 0, 2), ("o", 0), ("o", 1), ("q", 2),
    ("n", 1, 0), ("p", 1, 1), ("n", 0, 0), ("p", 1, 2), ("c",), ("p", 0, 3), ("n", 1, 2), ("n", 1, 1), ("n",
    0, 1), ("n", 0, 2), ("p", 1, 3), ("n", 0, 3), ("k", 0), ("m", 0, 0), ("m", 0, 1), ("m", 0, 2), ("m", 2,
    0), ("m", 2, 1), ("n", 1, 3), ("m", 0, 3), ("k", 1), ("m", 2, 2), ("m", 2, 3), ("m", 1, 0), ("m", 1, 1),
    ("m", 1, 2), ("m", 1, 3), ("m", 3, 0), ("m", 3, 1), ("m", 3, 2), ("m", 3, 3),
)


def place():
    role = lax.axis_index("role")
    ctx = lax.axis_index("ctx")
    return role, ctx // 8, (ctx // 2) % 4, ctx % 2


def ctx_of(z, y, core):
    return (z * 4 + y) * 2 + core


def remote(src, dst, send_sem, recv_sem, device):
    return pltpu.make_async_remote_copy(
        src_ref=src,
        dst_ref=dst,
        send_sem=send_sem,
        recv_sem=recv_sem,
        device_id=device,
        device_id_type=MESH,
    )


def pack(block, mark):
    head = mark.astype(jnp.bfloat16).astype(jnp.float32)
    rest = mark - head
    middle = rest.astype(jnp.bfloat16).astype(jnp.float32)
    last = rest - middle
    lane = lax.broadcasted_iota(jnp.int32, mark.shape[:-1] + (TAIL - LATENT,), mark.ndim - 1)
    tail = jnp.where(lane == 0, head, jnp.where(lane == 1, middle, jnp.where(lane == 2, last, 0.0)))
    return block.astype(jnp.bfloat16), tail.astype(jnp.bfloat16)


def mark_of(tail):
    return jnp.sum(tail.astype(jnp.float32), axis=-1, keepdims=True)


def joined(parts):
    marks = [mark_of(part[..., LATENT:]) for part in parts]
    best = functools.reduce(jnp.maximum, marks)
    weights = [jnp.exp2(mark - best) for mark in marks]
    amount = functools.reduce(jnp.add, weights)
    block = functools.reduce(
        jnp.add, [part[..., :LATENT].astype(jnp.float32) * w for part, w in zip(parts, weights)]
    )
    return block / amount, jnp.maximum(best + jnp.log2(amount), LOW)


def attend(queries, blocks, scale):
    scores = []
    for keys, live, flipped in blocks:
        inner = (0,) if flipped else (1,)
        score = lax.dot_general(
            queries, keys, (((1,), inner), ((), ())), preferred_element_type=jnp.float32
        )
        scores.append(jnp.where(live, score * scale, LOW))
    best = functools.reduce(
        jnp.maximum, [jnp.max(score, axis=1, keepdims=True) for score in scores]
    )
    best = jnp.maximum(best, FLOOR)
    amount, summed = 0.0, 0.0
    for score, (keys, _, flipped) in zip(scores, blocks):
        weight = jnp.exp2(score - best)
        amount = amount + jnp.sum(weight, axis=1, keepdims=True)
        latent, outer = (keys[:LATENT, :], (1,)) if flipped else (keys[:, :LATENT], (0,))
        summed = summed + lax.dot_general(
            weight.astype(jnp.bfloat16),
            latent,
            (((1,), outer), ((), ())),
            preferred_element_type=jnp.float32,
        )
    return best, amount, summed


def merge_two(first, second):
    best = jnp.maximum(first[0], second[0])
    one, two = jnp.exp2(first[0] - best), jnp.exp2(second[0] - best)
    return best, first[1] * one + second[1] * two, first[2] * one + second[2] * two


def kernel(
    scale,
    hidden_hbm,
    kv_hbm,
    gain_ref,
    nope_ref,
    rope_ref,
    key_up_ref,
    value_up_hbm,
    cache_hbm,
    length_ref,
    page_hbm,
    out_ref,
    hidden,
    weights,
    total,
    rows,
    queries,
    cache,
    value_up,
    pages,
    owner,
    old_best,
    old_amount,
    old_summed,
    outgoing,
    arrived,
    second,
    second_in,
    third,
    third_in,
    load_sem,
    kv_send,
    kv_recv,
    pair_send,
    pair_recv,
    q_send,
    q_recv,
    cache_send,
    cache_recv,
    rows_send,
    rows_recv,
    one_send,
    one_recv,
    two_send,
    two_recv,
    three_send,
    three_recv,
):
    x, z, y, core = place()
    depth = kv_hbm.shape[0]
    half = depth // 2
    chunk = depth * 8
    sibling = {"ctx": ctx_of(z, y, 1 - core)}

    barrier = pltpu.get_barrier_semaphore()
    pl.semaphore_signal(barrier, inc=1, device_id=sibling, device_id_type=MESH)
    for step in (1, 2, 3):
        for device in (
            {"role": (x + step) % 4},
            {"ctx": ctx_of((z + step) % 4, y, core)},
            {"ctx": ctx_of(z, (y + step) % 4, core)},
        ):
            pl.semaphore_signal(barrier, inc=1, device_id=device, device_id_type=MESH)

    line = [z, (z + 3) % 4, (z + 1) % 4, (z + 2) % 4]
    own_rows = pl.ds(pl.multiple_of(ctx_of(z, y, core) * depth, 16), depth)
    own_load = pltpu.make_async_copy(kv_hbm, weights.at[own_rows, :], load_sem.at[4])
    own_load.start()
    loads = []
    for index in range(4):
        columns = pl.ds(pl.multiple_of(line[index] * chunk, 128), chunk)
        loads.append(
            pltpu.make_async_copy(
                hidden_hbm.at[:, columns], hidden.at[:, columns], load_sem.at[index]
            )
        )
    page_start = pl.multiple_of((x * 16 + z * 4 + y) * pages.shape[1], 128)
    others = [
        pltpu.make_async_copy(
            page_hbm.at[:, pl.ds(page_start, pages.shape[1])], pages, load_sem.at[5]
        ),
        pltpu.make_async_copy(cache_hbm, cache.at[core], load_sem.at[6]),
        pltpu.make_async_copy(value_up_hbm, value_up, load_sem.at[7]),
    ]

    heads = key_up_ref.shape[0]
    row = lax.broadcasted_iota(jnp.int32, (16, 1), 0) % heads

    nope = jnp.concatenate(
        [nope_ref[r, t].astype(jnp.float32) for r in (0, 1) for t in (0, 1)], axis=0
    ).astype(jnp.bfloat16)
    rope = jnp.concatenate(
        [rope_ref[r, t].astype(jnp.float32) for r in (0, 1) for t in (0, 1)], axis=0
    )
    absorbed = jnp.zeros((16, LATENT), jnp.float32)
    for head in range(heads):
        product = jnp.dot(nope, key_up_ref[head], preferred_element_type=jnp.float32)
        absorbed = jnp.where(row == head, product, absorbed)
    queries[x, z, y, core, :, :LATENT] = absorbed.astype(jnp.bfloat16)
    queries[x, z, y, core, :, LATENT:] = rope.astype(jnp.bfloat16)
    own_load.wait()
    pl.semaphore_wait(barrier, 10)

    def piece(z_at, y_at, core_at, part):
        start = ctx_of(z_at, y_at, core_at) * depth + part * half
        return weights.at[pl.ds(pl.multiple_of(start, 16), half), :]

    def spot(part, first, second):
        return (second, first) if part == 0 else (first, second)

    mine = [(y, z), (z, y)]
    sends = []

    def begin(copy):
        copy.start()
        sends.append(copy)

    def send(part, slot, where, target):
        ref = piece(*spot(part, *where), core, part)
        device = {"ctx": ctx_of(*spot(part, *target), core)}
        begin(remote(ref, ref, kv_send.at[part, slot], kv_recv.at[part, slot], device))

    def pair(part, slot, where, core_at):
        ref = piece(*spot(part, *where), core_at, part)
        return remote(ref, ref, pair_send.at[part, slot], pair_recv.at[part, slot], sibling)

    def places(part):
        first, second = mine[part]
        along = [first, (first + 3) % 4, (first + 1) % 4, (first + 2) % 4]
        found = {15: (first, second)}
        for index in range(4):
            if index < 3:
                found[index] = (along[index + 1], second)
            found[3 + index] = (along[index], (second + 3) % 4)
            found[7 + index] = (along[index], (second + 1) % 4)
            found[11 + index] = (along[index], (second + 2) % 4)
        return found

    table = [places(0), places(1)]

    def pass_on(part, slot):
        begin(pair(part, slot, table[part][slot], core))

    seen = set()

    def need(part, *slots):
        for slot in slots:
            if (part, slot) not in seen and slot != 15:
                seen.add((part, slot))
                ref = piece(*spot(part, *table[part][slot]), core, part)
                remote(
                    ref, ref, kv_send.at[part, slot], kv_recv.at[part, slot], sibling
                ).wait_recv()
                pass_on(part, slot)

    def spread(part, index):
        first, second = mine[part]
        where = table[part][(15, 0, 1, 2)[index]]
        need(part, (15, 0, 1, 2)[index])
        send(part, 3 + index, where, (first, (second + 1) % 4))
        send(part, 7 + index, where, (first, (second + 3) % 4))

    def opposite(part):
        first, second = mine[part]
        turn = 1 - 2 * core
        need(part, 0, 1)
        send(part, 2, ((first - turn + 4) % 4, second), ((first + turn + 4) % 4, second))

    def onward(part, index):
        first, second = mine[part]
        slot, step = (3 + index, 1) if index in ONWARD else (7 + index, 3)
        need(part, slot)
        send(part, 11 + index, table[part][slot], (first, (second + step) % 4))

    one_at, two_at = jnp.where(core == 0, z, y), jnp.where(core == 0, y, z)

    def q_spot(first, second):
        return jnp.where(core == 0, first, second), jnp.where(core == 0, second, first)

    def q_copies(stage, step, sending):
        sign = 0 if sending else 4 - step
        if stage == 0:
            ref = queries.at[(x, *q_spot((one_at + sign) % 4, two_at), core)]
            device = {"ctx": ctx_of(*q_spot((one_at + step) % 4, two_at), core)}
            return [remote(ref, ref, q_send.at[0, step, 0], q_recv.at[0, step, 0], device)]
        if stage == 1:
            device = {"ctx": ctx_of(*q_spot(one_at, (two_at + step) % 4), core)}
            copies = []
            for index in range(4):
                ref = queries.at[
                    (x, *q_spot((one_at + index) % 4, (two_at + sign) % 4), core)
                ]
                copies.append(
                    remote(ref, ref, q_send.at[1, step, index], q_recv.at[1, step, index], device)
                )
            return copies
        ref = queries.at[(x + sign) % 4, :, :, core]
        device = {"role": (x + step) % 4}
        return [remote(ref, ref, q_send.at[2, step, 0], q_recv.at[2, step, 0], device)]

    def q_wait(stage):
        for step in (1, 3, 2):
            for copy in q_copies(stage, step, False):
                copy.wait_recv()

    def q_stage(stage):
        if stage > 0:
            q_wait(stage - 1)
        for step in (1, 3, 2):
            for copy in q_copies(stage, step, True):
                begin(copy)

    def multiply(index, tile):
        if tile == 0:
            slots = (
                (0, ((15, 0, 1, 2), (3, 4, 5, 6), (7, 8, 9, 10), (11, 12, 13, 14))[index]),
                (1, ((15, 0, 1, 2)[index], 3 + index, 7 + index, 11 + index)),
            )
            for part, group in slots:
                need(part, *group)
            for part, group in slots:
                for slot in group:
                    pair(part, slot, table[part][slot], 1 - core).wait_recv()
            loads[index].wait()
        columns = pl.ds(pl.multiple_of(line[index] * chunk, 128), chunk)
        down = pl.ds(pl.multiple_of(line[index] * chunk, 16), chunk)
        span = pl.ds(tile * 256, 256)
        product = jnp.dot(
            hidden[span, columns], weights[down, :], preferred_element_type=jnp.float32
        )
        if index == 0:
            total[span, :] = product
        else:
            total[span, :] += product

    def queries_of(group):
        return queries[group, :, :, core].reshape(256, 576)

    row_request = lax.broadcasted_iota(jnp.int32, (256, 1), 0) // 8 % 2

    def cache_pair(core_at):
        return remote(
            cache_hbm, cache.at[core_at], cache_send.at[0], cache_recv.at[0], sibling
        )

    def cached(turn):
        if turn == 0:
            others[1].wait()
        else:
            cache_pair(1 - core).wait_recv()
        source = core if turn == 0 else 1 - core
        slots = cache.shape[3]
        position = ctx_of(z, y, source) * slots + lax.broadcasted_iota(jnp.int32, (1, slots), 1)
        blocks = []
        for request in (0, 1):
            live = (position < length_ref[x * 2 + request]) & (row_request == request)
            blocks.append((cache[source, request], live, True))
        found = attend(queries_of(x), blocks, scale)
        if turn == 1:
            found = merge_two(found, (old_best[...], old_amount[...], old_summed[...]))
        old_best[...], old_amount[...], old_summed[...] = found

    for part in (0, 1):
        first, second_at = mine[part]
        send(part, 0, (first, second_at), ((first + 1) % 4, second_at))
        send(part, 1, (first, second_at), ((first + 3) % 4, second_at))
    for copy in others:
        copy.start()
    for load in loads:
        load.start()
    for part in (0, 1):
        pass_on(part, 15)

    for kind, *numbers in PLAN:
        if kind == "p":
            spread(*numbers)
        elif kind == "o":
            opposite(*numbers)
        elif kind == "n":
            onward(*numbers)
        elif kind == "q":
            q_stage(*numbers)
        elif kind == "c":
            begin(cache_pair(core))
        elif kind == "k":
            cached(*numbers)
        else:
            multiply(*numbers)

    def rows_pair(tile, core_at):
        ref = rows.at[core_at, pl.ds(tile * 256, 256), :]
        return remote(ref, ref, rows_send.at[tile], rows_recv.at[tile], sibling)

    for tile in range(4):
        span = pl.ds(tile * 256, 256)
        latent = total[span, :LATENT]
        inverse = lax.rsqrt(jnp.mean(latent * latent, axis=-1, keepdims=True) + 1e-06)
        rows[core, span, :LATENT] = (latent * inverse * gain_ref[...]).astype(jnp.bfloat16)
        rows[core, span, LATENT:] = total[span, LATENT:].astype(jnp.bfloat16)
        begin(rows_pair(tile, core))

    others[0].wait()
    bins = pages[...]
    request_of = (bins // 64 * 2 + bins % 2).astype(jnp.float32)
    count = pages.shape[1] // 2
    page = lax.broadcasted_iota(jnp.int32, (count, count * PAGE), 0)
    key = lax.broadcasted_iota(jnp.int32, (count, count * PAGE), 1)
    spread_out = (key // PAGE == page).astype(jnp.float32).astype(jnp.bfloat16)
    request_of = jnp.concatenate([request_of[:, :count], request_of[:, count:]], axis=0)
    wide = jnp.concatenate([request_of] * 4, axis=0).astype(jnp.bfloat16)
    owner[...] = jnp.dot(wide, spread_out, preferred_element_type=jnp.float32)[0:2, :]

    def compute(step):
        turn = TURNS[step]
        group = (x + turn) % 4
        if turn != 0:
            for copy in q_copies(2, 4 - turn, False):
                copy.wait_recv()
        if step == 0:
            for tile in range(4):
                rows_pair(tile, 1 - core).wait_recv()
        wanted = (group * 2 + row_request).astype(jnp.float32)
        blocks = []
        for source in (core, 1 - core):
            blocks.append((rows[source], owner[pl.ds(source, 1), :] == wanted, False))
        found = attend(queries_of(group), blocks, scale)
        if turn == 0:
            found = merge_two(found, (old_best[...], old_amount[...], old_summed[...]))
        best, amount, summed = found
        some = amount > 0.0
        amount = jnp.where(some, amount, 1.0)
        mark = jnp.where(some, best + jnp.log2(amount), LOW)
        block, tail = pack(summed / amount, mark)
        outgoing[step, :, :, :, :LATENT] = block.reshape(4, 4, 16, LATENT)
        outgoing[step, :, :, :, LATENT:] = tail.reshape(4, 4, 16, TAIL - LATENT)
        if turn != 0:

            @pl.when(core == 0)
            def _():
                out_x(step).start()

        @pl.when(core == 1)
        def _():
            for turn in (2, 1, 3):
                out_z(step, turn).start()

    def out_x(step):
        return remote(
            outgoing.at[step],
            arrived.at[step],
            one_send.at[step, 0],
            one_recv.at[step, 0],
            {"role": (x + TURNS[step]) % 4},
        )

    def out_z(step, turn):
        there = (z + turn) % 4
        return remote(
            outgoing.at[step, there],
            arrived.at[step, turn],
            one_send.at[step, turn],
            one_recv.at[step, turn],
            {"ctx": ctx_of(there, y, core)},
        )

    def next_y(turn):
        there = (y + turn) % 4
        return remote(
            second.at[:, there],
            second_in.at[turn],
            two_send.at[turn],
            two_recv.at[turn],
            {"ctx": ctx_of(z, there, core)},
        )

    def next_x(step):
        return remote(
            second.at[step],
            second_in.at[step],
            two_send.at[step],
            two_recv.at[step],
            {"role": (x + TURNS[step]) % 4},
        )

    def end_z(turn):
        there = (z + turn) % 4
        return remote(
            third.at[there],
            third_in.at[turn],
            three_send.at[turn],
            three_recv.at[turn],
            {"ctx": ctx_of(there, y, core)},
        )

    def end_y(turn):
        there = (y + turn) % 4
        return remote(
            third.at[there],
            third_in.at[turn],
            three_send.at[turn],
            three_recv.at[turn],
            {"ctx": ctx_of(z, there, core)},
        )

    def put(ref, parts):
        block, tail = pack(*joined(parts))
        ref[..., :LATENT] = block
        ref[..., LATENT:] = tail

    def merge(step):
        @pl.when(core == 1)
        def _():
            for turn in (1, 2, 3):
                out_z(step, turn).wait_recv()
            put(second.at[step], [outgoing[step, z]] + [arrived[step, turn] for turn in (1, 2, 3)])
            if TURNS[step] != 0:
                next_x(step).start()

    for step in range(4):
        compute(step)
        if step > 0:
            merge(step - 1)
    merge(3)

    def conclude(block):
        latent = block.astype(jnp.bfloat16)
        result = jnp.zeros((16, value_up.shape[2]), jnp.float32)
        for head in range(heads):
            product = jnp.dot(latent, value_up[head], preferred_element_type=jnp.float32)
            result = jnp.where(row == head, product, result)
        for index in range(4):
            out_ref[index // 2, index % 2] = result[index * 4 : index * 4 + 4].astype(jnp.bfloat16)

    others[2].wait()

    @pl.when(core == 0)
    def _():
        for step in range(3):
            out_x(step).wait_recv()
        put(second, [outgoing[3]] + [arrived[step] for step in range(3)])
        for turn in (2, 1, 3):
            next_y(turn).start()
        for turn in (1, 3, 2):
            next_y(turn).wait_recv()
        put(third, [second[:, y]] + [second_in[turn] for turn in (1, 2, 3)])
        for turn in (2, 1, 3):
            end_z(turn).start()
        for turn in (1, 3, 2):
            end_z(turn).wait_recv()
        conclude(joined([third[z]] + [third_in[turn] for turn in (1, 2, 3)])[0])
        for step in range(3):
            out_x(step).wait_send()
        for turn in (1, 2, 3):
            next_y(turn).wait_send()
            end_z(turn).wait_send()

    @pl.when(core == 1)
    def _():
        for step in range(3):
            next_x(step).wait_recv()
        put(third, [second[3]] + [second_in[step] for step in range(3)])
        for turn in (2, 1, 3):
            end_y(turn).start()
        for turn in (1, 3, 2):
            end_y(turn).wait_recv()
        conclude(joined([third[y]] + [third_in[turn] for turn in (1, 2, 3)])[0])
        for step in range(3):
            next_x(step).wait_send()
        for turn in (1, 2, 3):
            for step in range(4):
                out_z(step, turn).wait_send()
            end_y(turn).wait_send()

    for copy in sends:
        copy.wait_send()


def local(
    prefill_hidden,
    kv_down,
    kv_gain,
    q_nope,
    q_rope,
    key_up,
    value_up,
    latent_cache,
    cache_len,
    page_list,
):
    rows, width = prefill_hidden.shape[0], kv_down.shape[1]
    scale = math.log2(math.e) / math.sqrt(q_nope.shape[3] + q_rope.shape[3])
    vmem = pl.BlockSpec(memory_space=pltpu.VMEM)
    smem = pl.BlockSpec(memory_space=pltpu.SMEM)
    hbm = pl.BlockSpec(memory_space=pl.ANY)
    bf16, f32, dma = jnp.bfloat16, jnp.float32, pltpu.SemaphoreType.DMA
    flipped = jnp.swapaxes(latent_cache, 1, 2)
    return pl.pallas_call(
        functools.partial(kernel, scale),
        out_shape=jax.ShapeDtypeStruct(q_nope.shape[:3] + (value_up.shape[2],), bf16),
        in_specs=[hbm, hbm, vmem, vmem, vmem, vmem, hbm, hbm, smem, hbm],
        out_specs=vmem,
        scratch_shapes=[
            pltpu.VMEM(prefill_hidden.shape, bf16),
            pltpu.VMEM((prefill_hidden.shape[1], width), bf16),
            pltpu.VMEM((rows, width), f32),
            pltpu.VMEM((2, rows, width), bf16),
            pltpu.VMEM((4, 4, 4, 2, 16, width), bf16),
            pltpu.VMEM((2,) + flipped.shape, bf16),
            pltpu.VMEM(value_up.shape, bf16),
            pltpu.VMEM((1, 2 * rows // PAGE), jnp.int32),
            pltpu.VMEM((2, rows), f32),
            pltpu.VMEM((256, 1), f32),
            pltpu.VMEM((256, 1), f32),
            pltpu.VMEM((256, LATENT), f32),
            pltpu.VMEM((4, 4, 4, 16, TAIL), bf16),
            pltpu.VMEM((4, 4, 4, 16, TAIL), bf16),
            pltpu.VMEM((4, 4, 16, TAIL), bf16),
            pltpu.VMEM((4, 4, 16, TAIL), bf16),
            pltpu.VMEM((4, 16, TAIL), bf16),
            pltpu.VMEM((4, 16, TAIL), bf16),
            dma((8,)),
            dma((2, 15)),
            dma((2, 15)),
            dma((2, 16)),
            dma((2, 16)),
            dma((3, 4, 4)),
            dma((3, 4, 4)),
            dma((1,)),
            dma((1,)),
            dma((4,)),
            dma((4,)),
            dma((4, 4)),
            dma((4, 4)),
            dma((4,)),
            dma((4,)),
            dma((4,)),
            dma((4,)),
        ],
        compiler_params=pltpu.CompilerParams(
            collective_id=0, has_side_effects=True, vmem_limit_bytes=60 * 2**20
        ),
    )(
        prefill_hidden,
        kv_down,
        kv_gain.reshape(1, -1),
        q_nope,
        q_rope,
        key_up,
        value_up,
        flipped,
        cache_len,
        page_list.reshape(1, -1),
    )


def solution(mesh):
    return jax.shard_map(
        local,
        mesh=mesh,
        in_specs=(
            P(("role", "ctx"), None),
            P("ctx", None),
            P(),
            P("role", None, "ctx", None),
            P("role", None, "ctx", None),
            P("ctx", None, None),
            P("ctx", None, None),
            P("role", "ctx", None),
            P(),
            P(),
        ),
        out_specs=P("role", None, "ctx", None),
        check_vma=False,
    )
```

```python
import functools
import math

import jax
import jax.numpy as jnp
from jax import lax
from jax.experimental import pallas as pl
from jax.experimental.pallas import tpu as pltpu
from jax.sharding import PartitionSpec as P

LATENT = 512
PAGE = 4
LOW = -1e30
FLOOR = -1e29
TAIL = 640
MESH = pl.DeviceIdType.MESH
TURNS = (2, 1, 3, 0)
NEAR, SIDE, FAR = 1, 3, 2
RING = (0, NEAR, SIDE, FAR)
PLAN = (
    ("c",), ("q", 0), ("q", 1), ("p", 0, 0), ("p", 1, 0), ("p", 1, 2), ("o", 0), ("q", 2), ("p", 0, 1), ("w",
    0, 0), ("p", 0, 2), ("k", 0), ("o", 1), ("p", 1, 1), ("m", 0, 0, 0), ("n", 1, 2), ("w", 2, 0), ("m", 0, 0,
    1), ("n", 1, 0), ("p", 0, 3), ("k", 1), ("m", 2, 0, 0), ("m", 2, 0, 1), ("w", 1, 0), ("p", 1, 3), ("n", 0,
    0), ("n", 0, 3), ("m", 1, 0, 0), ("w", 0, 1), ("m", 1, 0, 1), ("n", 0, 1), ("n", 0, 2), ("n", 1, 1), ("w",
    2, 1), ("m", 0, 1, 0), ("n", 1, 3), ("m", 2, 1, 0), ("m", 0, 1, 1), ("m", 2, 1, 1), ("w", 3, 0), ("w", 1,
    1), ("w", 3, 1), ("m", 3, 0, 0), ("m", 1, 1, 0), ("m", 3, 0, 1), ("m", 1, 1, 1), ("m", 3, 1, 0), ("m", 3,
    1, 1),
)


def place():
    role = lax.axis_index("role")
    ctx = lax.axis_index("ctx")
    return role, ctx // 8, (ctx // 2) % 4, ctx % 2


def ctx_of(z, y, core):
    return (z * 4 + y) * 2 + core


def flip(place_at, turn):
    low = place_at % 2
    if turn == 0:
        return place_at
    if turn == FAR:
        return (place_at + 2) % 4
    return (place_at + (1 - 2 * low if turn == NEAR else 2 * low + 3)) % 4


def remote(src, dst, send_sem, recv_sem, device):
    return pltpu.make_async_remote_copy(
        src_ref=src,
        dst_ref=dst,
        send_sem=send_sem,
        recv_sem=recv_sem,
        device_id=device,
        device_id_type=MESH,
    )


def pack(block, mark):
    head = mark.astype(jnp.bfloat16).astype(jnp.float32)
    rest = mark - head
    middle = rest.astype(jnp.bfloat16).astype(jnp.float32)
    last = rest - middle
    lane = lax.broadcasted_iota(jnp.int32, mark.shape[:-1] + (TAIL - LATENT,), mark.ndim - 1)
    tail = jnp.where(lane == 0, head, jnp.where(lane == 1, middle, jnp.where(lane == 2, last, 0.0)))
    return block.astype(jnp.bfloat16), tail.astype(jnp.bfloat16)


def mark_of(tail):
    return jnp.sum(tail.astype(jnp.float32), axis=-1, keepdims=True)


def joined(parts):
    marks = [mark_of(part[..., LATENT:]) for part in parts]
    best = functools.reduce(jnp.maximum, marks)
    weights = [jnp.exp2(mark - best) for mark in marks]
    amount = functools.reduce(jnp.add, weights)
    block = functools.reduce(
        jnp.add, [part[..., :LATENT].astype(jnp.float32) * w for part, w in zip(parts, weights)]
    )
    return block / amount, jnp.maximum(best + jnp.log2(amount), LOW)


def attend(queries, blocks, scale):
    scores = []
    for keys, live, flipped in blocks:
        inner = (0,) if flipped else (1,)
        score = lax.dot_general(
            queries, keys, (((1,), inner), ((), ())), preferred_element_type=jnp.float32
        )
        scores.append(jnp.where(live, score * scale, LOW))
    best = functools.reduce(
        jnp.maximum, [jnp.max(score, axis=1, keepdims=True) for score in scores]
    )
    best = jnp.maximum(best, FLOOR)
    amount, summed = 0.0, 0.0
    for score, (keys, _, flipped) in zip(scores, blocks):
        weight = jnp.exp2(score - best)
        amount = amount + jnp.sum(weight, axis=1, keepdims=True)
        latent, outer = (keys[:LATENT, :], (1,)) if flipped else (keys[:, :LATENT], (0,))
        summed = summed + lax.dot_general(
            weight.astype(jnp.bfloat16),
            latent,
            (((1,), outer), ((), ())),
            preferred_element_type=jnp.float32,
        )
    return best, amount, summed


def merge_two(first, second):
    best = jnp.maximum(first[0], second[0])
    one, two = jnp.exp2(first[0] - best), jnp.exp2(second[0] - best)
    return best, first[1] * one + second[1] * two, first[2] * one + second[2] * two


def kernel(
    scale,
    hidden_hbm,
    kv_hbm,
    gain_ref,
    nope_ref,
    rope_ref,
    key_up_ref,
    value_up_hbm,
    cache_hbm,
    length_ref,
    page_hbm,
    out_ref,
    hidden,
    weights,
    total,
    rows,
    queries,
    cache,
    value_up,
    pages,
    owner,
    old_best,
    old_amount,
    old_summed,
    outgoing,
    arrived,
    second,
    second_in,
    third,
    third_in,
    load_sem,
    kv_send,
    kv_recv,
    pair_send,
    pair_recv,
    q_send,
    q_recv,
    cache_send,
    cache_recv,
    rows_send,
    rows_recv,
    one_send,
    one_recv,
    two_send,
    two_recv,
    three_send,
    three_recv,
):
    x, z, y, core = place()
    depth = kv_hbm.shape[0]
    half = depth // 2
    chunk = depth * 8
    sibling = {"ctx": ctx_of(z, y, 1 - core)}

    barrier = pltpu.get_barrier_semaphore()
    pl.semaphore_signal(barrier, inc=1, device_id=sibling, device_id_type=MESH)
    for step in (1, 2, 3):
        for device in (
            {"role": (x + step) % 4},
            {"ctx": ctx_of((z + step) % 4, y, core)},
            {"ctx": ctx_of(z, (y + step) % 4, core)},
        ):
            pl.semaphore_signal(barrier, inc=1, device_id=device, device_id_type=MESH)

    line = [flip(z, turn) for turn in RING]
    own_rows = pl.ds(pl.multiple_of(ctx_of(z, y, core) * depth, 16), depth)
    own_load = pltpu.make_async_copy(kv_hbm, weights.at[own_rows, :], load_sem.at[4])
    own_load.start()
    loads = []
    for index in range(4):
        columns = pl.ds(pl.multiple_of(line[index] * chunk, 128), chunk)
        loads.append(
            pltpu.make_async_copy(
                hidden_hbm.at[:, columns], hidden.at[:, columns], load_sem.at[index]
            )
        )
    page_start = pl.multiple_of((x * 16 + z * 4 + y) * pages.shape[1], 128)
    others = [
        pltpu.make_async_copy(
            page_hbm.at[:, pl.ds(page_start, pages.shape[1])], pages, load_sem.at[5]
        ),
        pltpu.make_async_copy(cache_hbm, cache.at[core], load_sem.at[6]),
        pltpu.make_async_copy(value_up_hbm, value_up, load_sem.at[7]),
    ]

    heads = key_up_ref.shape[0]
    row = lax.broadcasted_iota(jnp.int32, (16, 1), 0) % heads

    nope = jnp.concatenate(
        [nope_ref[r, t].astype(jnp.float32) for r in (0, 1) for t in (0, 1)], axis=0
    ).astype(jnp.bfloat16)
    rope = jnp.concatenate(
        [rope_ref[r, t].astype(jnp.float32) for r in (0, 1) for t in (0, 1)], axis=0
    )
    absorbed = jnp.zeros((16, LATENT), jnp.float32)
    for head in range(heads):
        product = jnp.dot(nope, key_up_ref[head], preferred_element_type=jnp.float32)
        absorbed = jnp.where(row == head, product, absorbed)
    queries[x, z, y, core, :, :LATENT] = absorbed.astype(jnp.bfloat16)
    queries[x, z, y, core, :, LATENT:] = rope.astype(jnp.bfloat16)
    own_load.wait()
    pl.semaphore_wait(barrier, 10)

    def piece(z_at, y_at, core_at, part):
        start = ctx_of(z_at, y_at, core_at) * depth + part * half
        return weights.at[pl.ds(pl.multiple_of(start, 16), half), :]

    def spot(part, first, second):
        return (second, first) if part == 0 else (first, second)

    mine = [(y, z), (z, y)]
    sends = []

    def begin(copy):
        copy.start()
        sends.append(copy)

    def send(part, slot, where, target):
        ref = piece(*spot(part, *where), core, part)
        device = {"ctx": ctx_of(*spot(part, *target), core)}
        begin(remote(ref, ref, kv_send.at[part, slot], kv_recv.at[part, slot], device))

    def pair(part, slot, where, core_at):
        ref = piece(*spot(part, *where), core_at, part)
        return remote(ref, ref, pair_send.at[part, slot], pair_recv.at[part, slot], sibling)

    def places(part):
        first, second = mine[part]
        along = [flip(first, turn) for turn in RING]
        found = {15: (first, second)}
        for index in range(4):
            if index < 3:
                found[index] = (along[index + 1], second)
            found[3 + index] = (along[index], flip(second, NEAR))
            found[7 + index] = (along[index], flip(second, SIDE))
            found[11 + index] = (along[index], flip(second, FAR))
        return found

    table = [places(0), places(1)]

    def pass_on(part, slot):
        begin(pair(part, slot, table[part][slot], core))

    seen = set()

    def need(part, *slots):
        for slot in slots:
            if (part, slot) not in seen and slot != 15:
                seen.add((part, slot))
                ref = piece(*spot(part, *table[part][slot]), core, part)
                remote(
                    ref, ref, kv_send.at[part, slot], kv_recv.at[part, slot], sibling
                ).wait_recv()
                pass_on(part, slot)

    def spread(part, index):
        first, second = mine[part]
        where = table[part][(15, 0, 1, 2)[index]]
        need(part, (15, 0, 1, 2)[index])
        send(part, 3 + index, where, (first, flip(second, NEAR)))
        send(part, 7 + index, where, (first, flip(second, SIDE)))

    def opposite(part):
        first, second = mine[part]
        need(part, 0, 1)
        source = jnp.where(core == 0, flip(first, NEAR), flip(first, SIDE))
        target = jnp.where(core == 0, flip(first, SIDE), flip(first, NEAR))
        send(part, 2, (source, second), (target, second))

    def onward(part, index):
        first, second = mine[part]
        slot, turn = (3 + index, SIDE) if index < 2 else (7 + index, NEAR)
        need(part, slot)
        send(part, 11 + index, table[part][slot], (first, flip(second, turn)))

    one_at, two_at = jnp.where(core == 0, z, y), jnp.where(core == 0, y, z)

    def q_spot(first, second):
        return jnp.where(core == 0, first, second), jnp.where(core == 0, second, first)

    def q_copies(stage, step, sending):
        sign = 0 if sending else 4 - step
        if stage == 0:
            ref = queries.at[(x, *q_spot((one_at + sign) % 4, two_at), core)]
            device = {"ctx": ctx_of(*q_spot((one_at + step) % 4, two_at), core)}
            return [remote(ref, ref, q_send.at[0, step, 0], q_recv.at[0, step, 0], device)]
        if stage == 1:
            device = {"ctx": ctx_of(*q_spot(one_at, (two_at + step) % 4), core)}
            copies = []
            for index in range(4):
                ref = queries.at[
                    (x, *q_spot((one_at + index) % 4, (two_at + sign) % 4), core)
                ]
                copies.append(
                    remote(ref, ref, q_send.at[1, step, index], q_recv.at[1, step, index], device)
                )
            return copies
        ref = queries.at[(x + sign) % 4, :, :, core]
        device = {"role": (x + step) % 4}
        return [remote(ref, ref, q_send.at[2, step, 0], q_recv.at[2, step, 0], device)]

    def q_wait(stage):
        for step in (1, 3, 2):
            for copy in q_copies(stage, step, False):
                copy.wait_recv()

    def q_stage(stage):
        if stage > 0:
            q_wait(stage - 1)
        for step in (1, 3, 2):
            for copy in q_copies(stage, step, True):
                begin(copy)

    loaded = set()

    def pieces_of(index, side):
        lines = (15, 0, 1, 2)
        base = (None, 3, 7, 11)[index]
        one = [lines[k] if index == 0 else base + k for k in ((0, 1), (2, 3))[side]]
        two = ((lines[index], 3 + index), (7 + index, 11 + index))[side]
        return [(0, slot) for slot in one] + [(1, slot) for slot in two]

    def gather(index, side):
        for part, slot in pieces_of(index, side):
            need(part, slot)

    def multiply(index, side, tile):
        if tile == 0:
            gather(index, side)
            for part, slot in pieces_of(index, side):
                pair(part, slot, table[part][slot], 1 - core).wait_recv()
            if index not in loaded:
                loaded.add(index)
                loads[index].wait()
        start = line[index] * chunk + (y // 2 if side == 0 else 1 - y // 2) * (chunk // 2)
        columns = pl.ds(pl.multiple_of(start, 128), chunk // 2)
        down = pl.ds(pl.multiple_of(start, 128), chunk // 2)
        span = pl.ds(tile * 512, 512)
        product = jnp.dot(
            hidden[span, columns], weights[down, :], preferred_element_type=jnp.float32
        )
        if index == 0 and side == 0:
            total[span, :] = product
        else:
            total[span, :] += product

    def queries_of(group):
        return queries[group, :, :, core].reshape(256, 576)

    row_request = lax.broadcasted_iota(jnp.int32, (256, 1), 0) // 8 % 2

    def cache_pair(core_at):
        return remote(
            cache_hbm, cache.at[core_at], cache_send.at[0], cache_recv.at[0], sibling
        )

    def cached(turn):
        if turn == 0:
            others[1].wait()
        else:
            cache_pair(1 - core).wait_recv()
        source = core if turn == 0 else 1 - core
        slots = cache.shape[3]
        position = ctx_of(z, y, source) * slots + lax.broadcasted_iota(jnp.int32, (1, slots), 1)
        blocks = []
        for request in (0, 1):
            live = (position < length_ref[x * 2 + request]) & (row_request == request)
            blocks.append((cache[source, request], live, True))
        found = attend(queries_of(x), blocks, scale)
        if turn == 1:
            found = merge_two(found, (old_best[...], old_amount[...], old_summed[...]))
        old_best[...], old_amount[...], old_summed[...] = found

    for part in (0, 1):
        first, second_at = mine[part]
        send(part, 0, (first, second_at), (flip(first, NEAR), second_at))
        send(part, 1, (first, second_at), (flip(first, SIDE), second_at))
    for copy in others:
        copy.start()
    for load in loads:
        load.start()
    for part in (0, 1):
        pass_on(part, 15)

    for kind, *numbers in PLAN:
        if kind == "p":
            spread(*numbers)
        elif kind == "o":
            opposite(*numbers)
        elif kind == "n":
            onward(*numbers)
        elif kind == "q":
            q_stage(*numbers)
        elif kind == "w":
            gather(*numbers)
        elif kind == "c":
            begin(cache_pair(core))
        elif kind == "k":
            cached(*numbers)
        else:
            multiply(*numbers)

    def rows_pair(tile, core_at):
        ref = rows.at[core_at, pl.ds(tile * 256, 256), :]
        return remote(ref, ref, rows_send.at[tile], rows_recv.at[tile], sibling)

    for tile in range(4):
        span = pl.ds(tile * 256, 256)
        latent = total[span, :LATENT]
        inverse = lax.rsqrt(jnp.mean(latent * latent, axis=-1, keepdims=True) + 1e-06)
        rows[core, span, :LATENT] = (latent * inverse * gain_ref[...]).astype(jnp.bfloat16)
        rows[core, span, LATENT:] = total[span, LATENT:].astype(jnp.bfloat16)
        begin(rows_pair(tile, core))

    others[0].wait()
    bins = pages[...]
    request_of = (bins // 64 * 2 + bins % 2).astype(jnp.float32)
    count = pages.shape[1] // 2
    page = lax.broadcasted_iota(jnp.int32, (count, count * PAGE), 0)
    key = lax.broadcasted_iota(jnp.int32, (count, count * PAGE), 1)
    spread_out = (key // PAGE == page).astype(jnp.float32).astype(jnp.bfloat16)
    request_of = jnp.concatenate([request_of[:, :count], request_of[:, count:]], axis=0)
    wide = jnp.concatenate([request_of] * 4, axis=0).astype(jnp.bfloat16)
    owner[...] = jnp.dot(wide, spread_out, preferred_element_type=jnp.float32)[0:2, :]

    def compute(step):
        turn = TURNS[step]
        group = (x + turn) % 4
        if turn != 0:
            for copy in q_copies(2, 4 - turn, False):
                copy.wait_recv()
        if step == 0:
            for tile in range(4):
                rows_pair(tile, 1 - core).wait_recv()
        wanted = (group * 2 + row_request).astype(jnp.float32)
        blocks = []
        for source in (core, 1 - core):
            blocks.append((rows[source], owner[pl.ds(source, 1), :] == wanted, False))
        found = attend(queries_of(group), blocks, scale)
        if turn == 0:
            found = merge_two(found, (old_best[...], old_amount[...], old_summed[...]))
        best, amount, summed = found
        some = amount > 0.0
        amount = jnp.where(some, amount, 1.0)
        mark = jnp.where(some, best + jnp.log2(amount), LOW)
        block, tail = pack(summed / amount, mark)
        outgoing[step, :, :, :, :LATENT] = block.reshape(4, 4, 16, LATENT)
        outgoing[step, :, :, :, LATENT:] = tail.reshape(4, 4, 16, TAIL - LATENT)
        if turn != 0:

            @pl.when(core == 0)
            def _():
                out_x(step).start()

        @pl.when(core == 1)
        def _():
            for turn in (2, 1, 3):
                out_z(step, turn).start()

    def out_x(step):
        return remote(
            outgoing.at[step],
            arrived.at[step],
            one_send.at[step, 0],
            one_recv.at[step, 0],
            {"role": (x + TURNS[step]) % 4},
        )

    def out_z(step, turn):
        there = (z + turn) % 4
        return remote(
            outgoing.at[step, there],
            arrived.at[step, turn],
            one_send.at[step, turn],
            one_recv.at[step, turn],
            {"ctx": ctx_of(there, y, core)},
        )

    def next_y(turn):
        there = (y + turn) % 4
        return remote(
            second.at[:, there],
            second_in.at[turn],
            two_send.at[turn],
            two_recv.at[turn],
            {"ctx": ctx_of(z, there, core)},
        )

    def next_x(step):
        return remote(
            second.at[step],
            second_in.at[step],
            two_send.at[step],
            two_recv.at[step],
            {"role": (x + TURNS[step]) % 4},
        )

    def end_z(turn):
        there = (z + turn) % 4
        return remote(
            third.at[there],
            third_in.at[turn],
            three_send.at[turn],
            three_recv.at[turn],
            {"ctx": ctx_of(there, y, core)},
        )

    def end_y(turn):
        there = (y + turn) % 4
        return remote(
            third.at[there],
            third_in.at[turn],
            three_send.at[turn],
            three_recv.at[turn],
            {"ctx": ctx_of(z, there, core)},
        )

    def put(ref, parts):
        block, tail = pack(*joined(parts))
        ref[..., :LATENT] = block
        ref[..., LATENT:] = tail

    def merge(step):
        @pl.when(core == 1)
        def _():
            for turn in (1, 2, 3):
                out_z(step, turn).wait_recv()
            put(second.at[step], [outgoing[step, z]] + [arrived[step, turn] for turn in (1, 2, 3)])
            if TURNS[step] != 0:
                next_x(step).start()

    for step in range(4):
        compute(step)
        if step > 0:
            merge(step - 1)
    merge(3)

    def conclude(block):
        latent = block.astype(jnp.bfloat16)
        result = jnp.zeros((16, value_up.shape[2]), jnp.float32)
        for head in range(heads):
            product = jnp.dot(latent, value_up[head], preferred_element_type=jnp.float32)
            result = jnp.where(row == head, product, result)
        for index in range(4):
            out_ref[index // 2, index % 2] = result[index * 4 : index * 4 + 4].astype(jnp.bfloat16)

    others[2].wait()

    @pl.when(core == 0)
    def _():
        for step in range(3):
            out_x(step).wait_recv()
        put(second, [outgoing[3]] + [arrived[step] for step in range(3)])
        for turn in (2, 1, 3):
            next_y(turn).start()
        for turn in (1, 3, 2):
            next_y(turn).wait_recv()
        put(third, [second[:, y]] + [second_in[turn] for turn in (1, 2, 3)])
        for turn in (2, 1, 3):
            end_z(turn).start()
        for turn in (1, 3, 2):
            end_z(turn).wait_recv()
        conclude(joined([third[z]] + [third_in[turn] for turn in (1, 2, 3)])[0])
        for step in range(3):
            out_x(step).wait_send()
        for turn in (1, 2, 3):
            next_y(turn).wait_send()
            end_z(turn).wait_send()

    @pl.when(core == 1)
    def _():
        for step in range(3):
            next_x(step).wait_recv()
        put(third, [second[3]] + [second_in[step] for step in range(3)])
        for turn in (2, 1, 3):
            end_y(turn).start()
        for turn in (1, 3, 2):
            end_y(turn).wait_recv()
        conclude(joined([third[y]] + [third_in[turn] for turn in (1, 2, 3)])[0])
        for step in range(3):
            next_x(step).wait_send()
        for turn in (1, 2, 3):
            for step in range(4):
                out_z(step, turn).wait_send()
            end_y(turn).wait_send()

    for copy in sends:
        copy.wait_send()


def local(
    prefill_hidden,
    kv_down,
    kv_gain,
    q_nope,
    q_rope,
    key_up,
    value_up,
    latent_cache,
    cache_len,
    page_list,
):
    rows, width = prefill_hidden.shape[0], kv_down.shape[1]
    scale = math.log2(math.e) / math.sqrt(q_nope.shape[3] + q_rope.shape[3])
    vmem = pl.BlockSpec(memory_space=pltpu.VMEM)
    smem = pl.BlockSpec(memory_space=pltpu.SMEM)
    hbm = pl.BlockSpec(memory_space=pl.ANY)
    bf16, f32, dma = jnp.bfloat16, jnp.float32, pltpu.SemaphoreType.DMA
    flipped = jnp.swapaxes(latent_cache, 1, 2)
    return pl.pallas_call(
        functools.partial(kernel, scale),
        out_shape=jax.ShapeDtypeStruct(q_nope.shape[:3] + (value_up.shape[2],), bf16),
        in_specs=[hbm, hbm, vmem, vmem, vmem, vmem, hbm, hbm, smem, hbm],
        out_specs=vmem,
        scratch_shapes=[
            pltpu.VMEM(prefill_hidden.shape, bf16),
            pltpu.VMEM((prefill_hidden.shape[1], width), bf16),
            pltpu.VMEM((rows, width), f32),
            pltpu.VMEM((2, rows, width), bf16),
            pltpu.VMEM((4, 4, 4, 2, 16, width), bf16),
            pltpu.VMEM((2,) + flipped.shape, bf16),
            pltpu.VMEM(value_up.shape, bf16),
            pltpu.VMEM((1, 2 * rows // PAGE), jnp.int32),
            pltpu.VMEM((2, rows), f32),
            pltpu.VMEM((256, 1), f32),
            pltpu.VMEM((256, 1), f32),
            pltpu.VMEM((256, LATENT), f32),
            pltpu.VMEM((4, 4, 4, 16, TAIL), bf16),
            pltpu.VMEM((4, 4, 4, 16, TAIL), bf16),
            pltpu.VMEM((4, 4, 16, TAIL), bf16),
            pltpu.VMEM((4, 4, 16, TAIL), bf16),
            pltpu.VMEM((4, 16, TAIL), bf16),
            pltpu.VMEM((4, 16, TAIL), bf16),
            dma((8,)),
            dma((2, 15)),
            dma((2, 15)),
            dma((2, 16)),
            dma((2, 16)),
            dma((3, 4, 4)),
            dma((3, 4, 4)),
            dma((1,)),
            dma((1,)),
            dma((4,)),
            dma((4,)),
            dma((4, 4)),
            dma((4, 4)),
            dma((4,)),
            dma((4,)),
            dma((4,)),
            dma((4,)),
        ],
        compiler_params=pltpu.CompilerParams(
            collective_id=0, has_side_effects=True, vmem_limit_bytes=60 * 2**20
        ),
    )(
        prefill_hidden,
        kv_down,
        kv_gain.reshape(1, -1),
        q_nope,
        q_rope,
        key_up,
        value_up,
        flipped,
        cache_len,
        page_list.reshape(1, -1),
    )


def solution(mesh):
    return jax.shard_map(
        local,
        mesh=mesh,
        in_specs=(
            P(("role", "ctx"), None),
            P("ctx", None),
            P(),
            P("role", None, "ctx", None),
            P("role", None, "ctx", None),
            P("ctx", None, None),
            P("ctx", None, None),
            P("role", "ctx", None),
            P(),
            P(),
        ),
        out_specs=P("role", None, "ctx", None),
        check_vma=False,
    )
```

```python
import functools
import math

import jax
import jax.numpy as jnp
from jax import lax
from jax.experimental import pallas as pl
from jax.experimental.pallas import tpu as pltpu
from jax.sharding import PartitionSpec as P

LATENT = 512
PAGE = 4
LOW = -1e30
FLOOR = -1e29
TAIL = 640
MESH = pl.DeviceIdType.MESH
TURNS = (2, 1, 3, 0)
NEAR, SIDE, FAR = 1, 3, 2
RING = (0, NEAR, SIDE, FAR)
PLAN = (
    ("c",), ("q", 0), ("q", 1), ("p", 0, 0), ("p", 1, 0), ("p", 1, 2), ("o", 0), ("q", 2), ("p", 0, 1), ("w",
    0, 0), ("p", 0, 2), ("k", 0), ("o", 1), ("p", 1, 1), ("m", 0, 0, 0), ("n", 1, 2), ("w", 2, 0), ("m", 0, 0,
    1), ("n", 1, 0), ("p", 0, 3), ("k", 1), ("m", 2, 0, 0), ("m", 2, 0, 1), ("w", 1, 0), ("p", 1, 3), ("n", 0,
    0), ("n", 0, 3), ("m", 1, 0, 0), ("w", 0, 1), ("m", 1, 0, 1), ("n", 0, 1), ("n", 0, 2), ("n", 1, 1), ("w",
    2, 1), ("m", 0, 1, 0), ("n", 1, 3), ("m", 2, 1, 0), ("m", 0, 1, 1), ("m", 2, 1, 1), ("w", 3, 0), ("w", 1,
    1), ("w", 3, 1), ("m", 3, 0, 0), ("m", 1, 1, 0), ("m", 3, 0, 1), ("m", 1, 1, 1), ("m", 3, 1, 0), ("m", 3,
    1, 1),
)


def place():
    role = lax.axis_index("role")
    ctx = lax.axis_index("ctx")
    return role, ctx // 8, (ctx // 2) % 4, ctx % 2


def ctx_of(z, y, core):
    return (z * 4 + y) * 2 + core


def flip(place_at, turn):
    low = place_at % 2
    if turn == 0:
        return place_at
    if turn == FAR:
        return (place_at + 2) % 4
    return (place_at + (1 - 2 * low if turn == NEAR else 2 * low + 3)) % 4


def remote(src, dst, send_sem, recv_sem, device):
    return pltpu.make_async_remote_copy(
        src_ref=src,
        dst_ref=dst,
        send_sem=send_sem,
        recv_sem=recv_sem,
        device_id=device,
        device_id_type=MESH,
    )


def pack(block, mark):
    head = mark.astype(jnp.bfloat16).astype(jnp.float32)
    rest = mark - head
    middle = rest.astype(jnp.bfloat16).astype(jnp.float32)
    last = rest - middle
    lane = lax.broadcasted_iota(jnp.int32, mark.shape[:-1] + (TAIL - LATENT,), mark.ndim - 1)
    tail = jnp.where(lane == 0, head, jnp.where(lane == 1, middle, jnp.where(lane == 2, last, 0.0)))
    return block.astype(jnp.bfloat16), tail.astype(jnp.bfloat16)


def mark_of(tail):
    return jnp.sum(tail.astype(jnp.float32), axis=-1, keepdims=True)


def joined(parts):
    marks = [mark_of(part[..., LATENT:]) for part in parts]
    best = functools.reduce(jnp.maximum, marks)
    weights = [jnp.exp2(mark - best) for mark in marks]
    amount = functools.reduce(jnp.add, weights)
    inverse = 1.0 / amount
    block = functools.reduce(
        jnp.add,
        [part[..., :LATENT].astype(jnp.float32) * (w * inverse) for part, w in zip(parts, weights)],
    )
    return block, jnp.maximum(best + jnp.log2(amount), LOW)


def attend(queries, blocks, scale):
    scores = []
    for keys, live, flipped in blocks:
        inner = (0,) if flipped else (1,)
        score = lax.dot_general(
            queries, keys, (((1,), inner), ((), ())), preferred_element_type=jnp.float32
        )
        scores.append(jnp.where(live, score * scale, LOW))
    best = functools.reduce(
        jnp.maximum, [jnp.max(score, axis=1, keepdims=True) for score in scores]
    )
    best = jnp.maximum(best, FLOOR)
    amount, summed = 0.0, 0.0
    for score, (keys, _, flipped) in zip(scores, blocks):
        weight = jnp.exp2(score - best)
        amount = amount + jnp.sum(weight, axis=1, keepdims=True)
        latent, outer = (keys[:LATENT, :], (1,)) if flipped else (keys[:, :LATENT], (0,))
        summed = summed + lax.dot_general(
            weight.astype(jnp.bfloat16),
            latent,
            (((1,), outer), ((), ())),
            preferred_element_type=jnp.float32,
        )
    return best, amount, summed


def merge_two(first, second):
    best = jnp.maximum(first[0], second[0])
    one, two = jnp.exp2(first[0] - best), jnp.exp2(second[0] - best)
    return best, first[1] * one + second[1] * two, first[2] * one + second[2] * two


def kernel(
    scale,
    hidden_hbm,
    kv_hbm,
    gain_ref,
    nope_ref,
    rope_ref,
    key_up_ref,
    value_up_hbm,
    cache_hbm,
    length_ref,
    page_hbm,
    out_ref,
    hidden,
    weights,
    total,
    rows,
    queries,
    cache,
    value_up,
    pages,
    owner,
    old_best,
    old_amount,
    old_summed,
    outgoing,
    arrived,
    second,
    second_in,
    third,
    third_in,
    load_sem,
    kv_send,
    kv_recv,
    pair_send,
    pair_recv,
    q_send,
    q_recv,
    cache_send,
    cache_recv,
    rows_send,
    rows_recv,
    one_send,
    one_recv,
    two_send,
    two_recv,
    three_send,
    three_recv,
):
    x, z, y, core = place()
    depth = kv_hbm.shape[0]
    half = depth // 2
    chunk = depth * 8
    sibling = {"ctx": ctx_of(z, y, 1 - core)}

    barrier = pltpu.get_barrier_semaphore()
    pl.semaphore_signal(barrier, inc=1, device_id=sibling, device_id_type=MESH)
    for step in (1, 2, 3):
        for device in (
            {"role": (x + step) % 4},
            {"ctx": ctx_of((z + step) % 4, y, core)},
            {"ctx": ctx_of(z, (y + step) % 4, core)},
        ):
            pl.semaphore_signal(barrier, inc=1, device_id=device, device_id_type=MESH)

    line = [flip(z, turn) for turn in RING]
    own_rows = pl.ds(pl.multiple_of(ctx_of(z, y, core) * depth, 16), depth)
    own_load = pltpu.make_async_copy(kv_hbm, weights.at[own_rows, :], load_sem.at[4])
    own_load.start()
    loads = []
    for index in range(4):
        columns = pl.ds(pl.multiple_of(line[index] * chunk, 128), chunk)
        loads.append(
            pltpu.make_async_copy(
                hidden_hbm.at[:, columns], hidden.at[:, columns], load_sem.at[index]
            )
        )
    page_start = pl.multiple_of((x * 16 + z * 4 + y) * pages.shape[1], 128)
    others = [
        pltpu.make_async_copy(
            page_hbm.at[:, pl.ds(page_start, pages.shape[1])], pages, load_sem.at[5]
        ),
        pltpu.make_async_copy(cache_hbm, cache.at[core], load_sem.at[6]),
        pltpu.make_async_copy(value_up_hbm, value_up, load_sem.at[7]),
    ]

    heads = key_up_ref.shape[0]
    row = lax.broadcasted_iota(jnp.int32, (16, 1), 0) % heads

    nope = jnp.concatenate(
        [nope_ref[r, t].astype(jnp.float32) for r in (0, 1) for t in (0, 1)], axis=0
    ).astype(jnp.bfloat16)
    rope = jnp.concatenate(
        [rope_ref[r, t].astype(jnp.float32) for r in (0, 1) for t in (0, 1)], axis=0
    )
    absorbed = jnp.zeros((16, LATENT), jnp.float32)
    for head in range(heads):
        product = jnp.dot(nope, key_up_ref[head], preferred_element_type=jnp.float32)
        absorbed = jnp.where(row == head, product, absorbed)
    queries[x, z, y, core, :, :LATENT] = absorbed.astype(jnp.bfloat16)
    queries[x, z, y, core, :, LATENT:] = rope.astype(jnp.bfloat16)
    own_load.wait()
    pl.semaphore_wait(barrier, 10)

    def piece(z_at, y_at, core_at, part):
        start = ctx_of(z_at, y_at, core_at) * depth + part * half
        return weights.at[pl.ds(pl.multiple_of(start, 16), half), :]

    def spot(part, first, second):
        return (second, first) if part == 0 else (first, second)

    mine = [(y, z), (z, y)]
    sends = []

    def begin(copy):
        copy.start()
        sends.append(copy)

    def send(part, slot, where, target):
        ref = piece(*spot(part, *where), core, part)
        device = {"ctx": ctx_of(*spot(part, *target), core)}
        begin(remote(ref, ref, kv_send.at[part, slot], kv_recv.at[part, slot], device))

    def pair(part, slot, where, core_at):
        ref = piece(*spot(part, *where), core_at, part)
        return remote(ref, ref, pair_send.at[part, slot], pair_recv.at[part, slot], sibling)

    def places(part):
        first, second = mine[part]
        along = [flip(first, turn) for turn in RING]
        found = {15: (first, second)}
        for index in range(4):
            if index < 3:
                found[index] = (along[index + 1], second)
            found[3 + index] = (along[index], flip(second, NEAR))
            found[7 + index] = (along[index], flip(second, SIDE))
            found[11 + index] = (along[index], flip(second, FAR))
        return found

    table = [places(0), places(1)]

    def pass_on(part, slot):
        begin(pair(part, slot, table[part][slot], core))

    seen = set()

    def need(part, *slots):
        for slot in slots:
            if (part, slot) not in seen and slot != 15:
                seen.add((part, slot))
                ref = piece(*spot(part, *table[part][slot]), core, part)
                remote(
                    ref, ref, kv_send.at[part, slot], kv_recv.at[part, slot], sibling
                ).wait_recv()
                pass_on(part, slot)

    def spread(part, index):
        first, second = mine[part]
        where = table[part][(15, 0, 1, 2)[index]]
        need(part, (15, 0, 1, 2)[index])
        send(part, 3 + index, where, (first, flip(second, NEAR)))
        send(part, 7 + index, where, (first, flip(second, SIDE)))

    def opposite(part):
        first, second = mine[part]
        need(part, 0, 1)
        source = jnp.where(core == 0, flip(first, NEAR), flip(first, SIDE))
        target = jnp.where(core == 0, flip(first, SIDE), flip(first, NEAR))
        send(part, 2, (source, second), (target, second))

    def onward(part, index):
        first, second = mine[part]
        slot, turn = (3 + index, SIDE) if index < 2 else (7 + index, NEAR)
        need(part, slot)
        send(part, 11 + index, table[part][slot], (first, flip(second, turn)))

    one_at, two_at = jnp.where(core == 0, z, y), jnp.where(core == 0, y, z)

    def q_spot(first, second):
        return jnp.where(core == 0, first, second), jnp.where(core == 0, second, first)

    def q_copies(stage, step, sending):
        sign = 0 if sending else 4 - step
        if stage == 0:
            ref = queries.at[(x, *q_spot((one_at + sign) % 4, two_at), core)]
            device = {"ctx": ctx_of(*q_spot((one_at + step) % 4, two_at), core)}
            return [remote(ref, ref, q_send.at[0, step, 0], q_recv.at[0, step, 0], device)]
        if stage == 1:
            device = {"ctx": ctx_of(*q_spot(one_at, (two_at + step) % 4), core)}
            copies = []
            for index in range(4):
                ref = queries.at[
                    (x, *q_spot((one_at + index) % 4, (two_at + sign) % 4), core)
                ]
                copies.append(
                    remote(ref, ref, q_send.at[1, step, index], q_recv.at[1, step, index], device)
                )
            return copies
        ref = queries.at[(x + sign) % 4, :, :, core]
        device = {"role": (x + step) % 4}
        return [remote(ref, ref, q_send.at[2, step, 0], q_recv.at[2, step, 0], device)]

    def q_wait(stage):
        for step in (1, 3, 2):
            for copy in q_copies(stage, step, False):
                copy.wait_recv()

    def q_stage(stage):
        if stage > 0:
            q_wait(stage - 1)
        for step in (1, 3, 2):
            for copy in q_copies(stage, step, True):
                begin(copy)

    loaded = set()

    def pieces_of(index, side):
        lines = (15, 0, 1, 2)
        base = (None, 3, 7, 11)[index]
        one = [lines[k] if index == 0 else base + k for k in ((0, 1), (2, 3))[side]]
        two = ((lines[index], 3 + index), (7 + index, 11 + index))[side]
        return [(0, slot) for slot in one] + [(1, slot) for slot in two]

    def gather(index, side):
        for part, slot in pieces_of(index, side):
            need(part, slot)

    def multiply(index, side, tile):
        if tile == 0:
            gather(index, side)
            for part, slot in pieces_of(index, side):
                pair(part, slot, table[part][slot], 1 - core).wait_recv()
            if index not in loaded:
                loaded.add(index)
                loads[index].wait()
        start = line[index] * chunk + (y // 2 if side == 0 else 1 - y // 2) * (chunk // 2)
        columns = pl.ds(pl.multiple_of(start, 128), chunk // 2)
        down = pl.ds(pl.multiple_of(start, 128), chunk // 2)
        span = pl.ds(tile * 512, 512)
        product = jnp.dot(
            hidden[span, columns], weights[down, :], preferred_element_type=jnp.float32
        )
        if index == 0 and side == 0:
            total[span, :] = product
        else:
            total[span, :] += product

    def queries_of(group):
        return queries[group, :, :, core].reshape(256, 576)

    row_request = lax.broadcasted_iota(jnp.int32, (256, 1), 0) // 8 % 2

    def cache_pair(core_at):
        return remote(
            cache_hbm, cache.at[core_at], cache_send.at[0], cache_recv.at[0], sibling
        )

    def cached(turn):
        if turn == 0:
            others[1].wait()
        else:
            cache_pair(1 - core).wait_recv()
        source = core if turn == 0 else 1 - core
        slots = cache.shape[3]
        position = ctx_of(z, y, source) * slots + lax.broadcasted_iota(jnp.int32, (1, slots), 1)
        blocks = []
        for request in (0, 1):
            live = (position < length_ref[x * 2 + request]) & (row_request == request)
            blocks.append((cache[source, request], live, True))
        found = attend(queries_of(x), blocks, scale)
        if turn == 1:
            found = merge_two(found, (old_best[...], old_amount[...], old_summed[...]))
        old_best[...], old_amount[...], old_summed[...] = found

    for part in (0, 1):
        first, second_at = mine[part]
        send(part, 0, (first, second_at), (flip(first, NEAR), second_at))
        send(part, 1, (first, second_at), (flip(first, SIDE), second_at))
    for copy in others:
        copy.start()
    for load in loads:
        load.start()
    for part in (0, 1):
        pass_on(part, 15)

    for kind, *numbers in PLAN:
        if kind == "p":
            spread(*numbers)
        elif kind == "o":
            opposite(*numbers)
        elif kind == "n":
            onward(*numbers)
        elif kind == "q":
            q_stage(*numbers)
        elif kind == "w":
            gather(*numbers)
        elif kind == "c":
            begin(cache_pair(core))
        elif kind == "k":
            cached(*numbers)
        else:
            multiply(*numbers)

    def rows_pair(tile, core_at):
        ref = rows.at[core_at, pl.ds(tile * 256, 256), :]
        return remote(ref, ref, rows_send.at[tile], rows_recv.at[tile], sibling)

    for tile in range(4):
        span = pl.ds(tile * 256, 256)
        latent = total[span, :LATENT]
        inverse = lax.rsqrt(jnp.mean(latent * latent, axis=-1, keepdims=True) + 1e-06)
        rows[core, span, :LATENT] = (latent * inverse * gain_ref[...]).astype(jnp.bfloat16)
        rows[core, span, LATENT:] = total[span, LATENT:].astype(jnp.bfloat16)
        begin(rows_pair(tile, core))

    others[0].wait()
    bins = pages[...]
    request_of = (bins // 64 * 2 + bins % 2).astype(jnp.float32)
    count = pages.shape[1] // 2
    page = lax.broadcasted_iota(jnp.int32, (count, count * PAGE), 0)
    key = lax.broadcasted_iota(jnp.int32, (count, count * PAGE), 1)
    spread_out = (key // PAGE == page).astype(jnp.float32).astype(jnp.bfloat16)
    request_of = jnp.concatenate([request_of[:, :count], request_of[:, count:]], axis=0)
    wide = jnp.concatenate([request_of] * 4, axis=0).astype(jnp.bfloat16)
    owner[...] = jnp.dot(wide, spread_out, preferred_element_type=jnp.float32)[0:2, :]

    def compute(step):
        turn = TURNS[step]
        group = (x + turn) % 4
        if turn != 0:
            for copy in q_copies(2, 4 - turn, False):
                copy.wait_recv()
        if step == 0:
            for tile in range(4):
                rows_pair(tile, 1 - core).wait_recv()
        wanted = (group * 2 + row_request).astype(jnp.float32)
        blocks = []
        for source in (core, 1 - core):
            blocks.append((rows[source], owner[pl.ds(source, 1), :] == wanted, False))
        found = attend(queries_of(group), blocks, scale)
        if turn == 0:
            found = merge_two(found, (old_best[...], old_amount[...], old_summed[...]))
        best, amount, summed = found
        some = amount > 0.0
        amount = jnp.where(some, amount, 1.0)
        mark = jnp.where(some, best + jnp.log2(amount), LOW)
        block, tail = pack(summed * (1.0 / amount), mark)
        outgoing[step, :, :, :, :LATENT] = block.reshape(4, 4, 16, LATENT)
        outgoing[step, :, :, :, LATENT:] = tail.reshape(4, 4, 16, TAIL - LATENT)

        @pl.when(core == 0)
        def _():
            for turn in (2, 1, 3):
                out_y(step, turn).start()

        @pl.when(core == 1)
        def _():
            for turn in (2, 1, 3):
                out_z(step, turn).start()

    def out_y(step, turn):
        there = (y + turn) % 4
        return remote(
            outgoing.at[step, :, there],
            arrived.at[step, turn],
            one_send.at[step, turn],
            one_recv.at[step, turn],
            {"ctx": ctx_of(z, there, core)},
        )

    def out_z(step, turn):
        there = (z + turn) % 4
        return remote(
            outgoing.at[step, there],
            arrived.at[step, turn],
            one_send.at[step, turn],
            one_recv.at[step, turn],
            {"ctx": ctx_of(there, y, core)},
        )

    def next_x(step):
        return remote(
            second.at[step],
            second_in.at[step],
            two_send.at[step],
            two_recv.at[step],
            {"role": (x + TURNS[step]) % 4},
        )

    def end_z(turn):
        there = (z + turn) % 4
        return remote(
            third.at[there],
            third_in.at[turn],
            three_send.at[turn],
            three_recv.at[turn],
            {"ctx": ctx_of(there, y, core)},
        )

    def end_y(turn):
        there = (y + turn) % 4
        return remote(
            third.at[there],
            third_in.at[turn],
            three_send.at[turn],
            three_recv.at[turn],
            {"ctx": ctx_of(z, there, core)},
        )

    def put(ref, parts):
        block, tail = pack(*joined(parts))
        ref[..., :LATENT] = block
        ref[..., LATENT:] = tail

    def merge(step):
        @pl.when(core == 0)
        def _():
            for turn in (1, 3, 2):
                out_y(step, turn).wait_recv()

        @pl.when(core == 1)
        def _():
            for turn in (1, 3, 2):
                out_z(step, turn).wait_recv()

        own = jnp.where(core == 0, outgoing[step, :, y], outgoing[step, z])
        put(second.at[step], [own] + [arrived[step, turn] for turn in (1, 2, 3)])
        if TURNS[step] != 0:
            next_x(step).start()

    for step in range(4):
        compute(step)
        if step > 0:
            merge(step - 1)
    merge(3)

    def conclude(block):
        latent = block.astype(jnp.bfloat16)
        result = jnp.zeros((16, value_up.shape[2]), jnp.float32)
        for head in range(heads):
            product = jnp.dot(latent, value_up[head], preferred_element_type=jnp.float32)
            result = jnp.where(row == head, product, result)
        for index in range(4):
            out_ref[index // 2, index % 2] = result[index * 4 : index * 4 + 4].astype(jnp.bfloat16)

    others[2].wait()
    for step in range(3):
        next_x(step).wait_recv()
    put(third, [second[3]] + [second_in[step] for step in range(3)])

    @pl.when(core == 0)
    def _():
        for turn in (2, 1, 3):
            end_z(turn).start()
        for turn in (1, 3, 2):
            end_z(turn).wait_recv()

    @pl.when(core == 1)
    def _():
        for turn in (2, 1, 3):
            end_y(turn).start()
        for turn in (1, 3, 2):
            end_y(turn).wait_recv()

    own = jnp.where(core == 0, third[z], third[y])
    conclude(joined([own] + [third_in[turn] for turn in (1, 2, 3)])[0])

    for step in range(3):
        next_x(step).wait_send()

    @pl.when(core == 0)
    def _():
        for turn in (1, 2, 3):
            for step in range(4):
                out_y(step, turn).wait_send()
            end_z(turn).wait_send()

    @pl.when(core == 1)
    def _():
        for turn in (1, 2, 3):
            for step in range(4):
                out_z(step, turn).wait_send()
            end_y(turn).wait_send()

    for copy in sends:
        copy.wait_send()


def local(
    prefill_hidden,
    kv_down,
    kv_gain,
    q_nope,
    q_rope,
    key_up,
    value_up,
    latent_cache,
    cache_len,
    page_list,
):
    rows, width = prefill_hidden.shape[0], kv_down.shape[1]
    scale = math.log2(math.e) / math.sqrt(q_nope.shape[3] + q_rope.shape[3])
    vmem = pl.BlockSpec(memory_space=pltpu.VMEM)
    smem = pl.BlockSpec(memory_space=pltpu.SMEM)
    hbm = pl.BlockSpec(memory_space=pl.ANY)
    bf16, f32, dma = jnp.bfloat16, jnp.float32, pltpu.SemaphoreType.DMA
    flipped = jnp.swapaxes(latent_cache, 1, 2)
    return pl.pallas_call(
        functools.partial(kernel, scale),
        out_shape=jax.ShapeDtypeStruct(q_nope.shape[:3] + (value_up.shape[2],), bf16),
        in_specs=[hbm, hbm, vmem, vmem, vmem, vmem, hbm, hbm, smem, hbm],
        out_specs=vmem,
        scratch_shapes=[
            pltpu.VMEM(prefill_hidden.shape, bf16),
            pltpu.VMEM((prefill_hidden.shape[1], width), bf16),
            pltpu.VMEM((rows, width), f32),
            pltpu.VMEM((2, rows, width), bf16),
            pltpu.VMEM((4, 4, 4, 2, 16, width), bf16),
            pltpu.VMEM((2,) + flipped.shape, bf16),
            pltpu.VMEM(value_up.shape, bf16),
            pltpu.VMEM((1, 2 * rows // PAGE), jnp.int32),
            pltpu.VMEM((2, rows), f32),
            pltpu.VMEM((256, 1), f32),
            pltpu.VMEM((256, 1), f32),
            pltpu.VMEM((256, LATENT), f32),
            pltpu.VMEM((4, 4, 4, 16, TAIL), bf16),
            pltpu.VMEM((4, 4, 4, 16, TAIL), bf16),
            pltpu.VMEM((4, 4, 16, TAIL), bf16),
            pltpu.VMEM((4, 4, 16, TAIL), bf16),
            pltpu.VMEM((4, 16, TAIL), bf16),
            pltpu.VMEM((4, 16, TAIL), bf16),
            dma((8,)),
            dma((2, 15)),
            dma((2, 15)),
            dma((2, 16)),
            dma((2, 16)),
            dma((3, 4, 4)),
            dma((3, 4, 4)),
            dma((1,)),
            dma((1,)),
            dma((4,)),
            dma((4,)),
            dma((4, 4)),
            dma((4, 4)),
            dma((4,)),
            dma((4,)),
            dma((4,)),
            dma((4,)),
        ],
        compiler_params=pltpu.CompilerParams(
            collective_id=0, has_side_effects=True, vmem_limit_bytes=60 * 2**20
        ),
    )(
        prefill_hidden,
        kv_down,
        kv_gain.reshape(1, -1),
        q_nope,
        q_rope,
        key_up,
        value_up,
        flipped,
        cache_len,
        page_list.reshape(1, -1),
    )


def solution(mesh):
    return jax.shard_map(
        local,
        mesh=mesh,
        in_specs=(
            P(("role", "ctx"), None),
            P("ctx", None),
            P(),
            P("role", None, "ctx", None),
            P("role", None, "ctx", None),
            P("ctx", None, None),
            P("ctx", None, None),
            P("role", "ctx", None),
            P(),
            P(),
        ),
        out_specs=P("role", None, "ctx", None),
        check_vma=False,
    )
```

```python
import functools
import math

import jax
import jax.numpy as jnp
from jax import lax
from jax.experimental import pallas as pl
from jax.experimental.pallas import tpu as pltpu
from jax.sharding import PartitionSpec as P

LATENT = 512
PAGE = 4
LOW = -1e30
FLOOR = -1e29
TAIL = 640
MESH = pl.DeviceIdType.MESH
TURNS = (2, 1, 3, 0)
NEAR, SIDE, FAR = 1, 3, 2
RING = (0, NEAR, SIDE, FAR)
PLAN = (
    ("c",), ("q", 0), ("q", 1), ("p", 0, 0), ("p", 1, 0), ("p", 1, 2), ("o", 0), ("q", 2), ("p", 0, 1), ("w",
    0, 0), ("p", 0, 2), ("k", 0), ("o", 1), ("p", 1, 1), ("m", 0, 0, 0), ("n", 1, 2), ("w", 2, 0), ("m", 0, 0,
    1), ("n", 1, 0), ("p", 0, 3), ("k", 1), ("m", 2, 0, 0), ("m", 2, 0, 1), ("w", 1, 0), ("p", 1, 3), ("n", 0,
    0), ("n", 0, 3), ("m", 1, 0, 0), ("w", 0, 1), ("m", 1, 0, 1), ("n", 0, 1), ("n", 0, 2), ("n", 1, 1), ("w",
    2, 1), ("m", 0, 1, 0), ("n", 1, 3), ("m", 2, 1, 0), ("m", 0, 1, 1), ("m", 2, 1, 1), ("w", 3, 0), ("w", 1,
    1), ("w", 3, 1), ("m", 3, 0, 0), ("m", 1, 1, 0), ("m", 3, 0, 1), ("m", 1, 1, 1), ("m", 3, 1, 0), ("m", 3,
    1, 1),
)


def place():
    role = lax.axis_index("role")
    ctx = lax.axis_index("ctx")
    return role, ctx // 8, (ctx // 2) % 4, ctx % 2


def ctx_of(z, y, core):
    return (z * 4 + y) * 2 + core


def flip(place_at, turn):
    low = place_at % 2
    if turn == 0:
        return place_at
    if turn == FAR:
        return (place_at + 2) % 4
    return (place_at + (1 - 2 * low if turn == NEAR else 2 * low + 3)) % 4


def remote(src, dst, send_sem, recv_sem, device):
    return pltpu.make_async_remote_copy(
        src_ref=src,
        dst_ref=dst,
        send_sem=send_sem,
        recv_sem=recv_sem,
        device_id=device,
        device_id_type=MESH,
    )


def pack(block, mark):
    head = mark.astype(jnp.bfloat16).astype(jnp.float32)
    rest = mark - head
    middle = rest.astype(jnp.bfloat16).astype(jnp.float32)
    last = rest - middle
    lane = lax.broadcasted_iota(jnp.int32, mark.shape[:-1] + (TAIL - LATENT,), mark.ndim - 1)
    tail = jnp.where(lane == 0, head, jnp.where(lane == 1, middle, jnp.where(lane == 2, last, 0.0)))
    return block.astype(jnp.bfloat16), tail.astype(jnp.bfloat16)


def mark_of(tail):
    return jnp.sum(tail.astype(jnp.float32), axis=-1, keepdims=True)


def joined(parts):
    marks = [mark_of(part[..., LATENT:]) for part in parts]
    best = functools.reduce(jnp.maximum, marks)
    weights = [jnp.exp2(mark - best) for mark in marks]
    amount = functools.reduce(jnp.add, weights)
    inverse = 1.0 / amount
    block = functools.reduce(
        jnp.add,
        [part[..., :LATENT].astype(jnp.float32) * (w * inverse) for part, w in zip(parts, weights)],
    )
    return block, jnp.maximum(best + jnp.log2(amount), LOW)


def attend(queries, blocks, scale):
    scores = []
    for keys, live, flipped in blocks:
        inner = (0,) if flipped else (1,)
        score = lax.dot_general(
            queries, keys, (((1,), inner), ((), ())), preferred_element_type=jnp.float32
        )
        scores.append(jnp.where(live, score * scale, LOW))
    best = functools.reduce(
        jnp.maximum, [jnp.max(score, axis=1, keepdims=True) for score in scores]
    )
    best = jnp.maximum(best, FLOOR)
    amount, summed = 0.0, 0.0
    for score, (keys, _, flipped) in zip(scores, blocks):
        weight = jnp.exp2(score - best)
        amount = amount + jnp.sum(weight, axis=1, keepdims=True)
        latent, outer = (keys[:LATENT, :], (1,)) if flipped else (keys[:, :LATENT], (0,))
        summed = summed + lax.dot_general(
            weight.astype(jnp.bfloat16),
            latent,
            (((1,), outer), ((), ())),
            preferred_element_type=jnp.float32,
        )
    return best, amount, summed


def merge_two(first, second):
    best = jnp.maximum(first[0], second[0])
    one, two = jnp.exp2(first[0] - best), jnp.exp2(second[0] - best)
    return best, first[1] * one + second[1] * two, first[2] * one + second[2] * two


def kernel(
    scale,
    hidden_hbm,
    kv_hbm,
    gain_ref,
    nope_ref,
    rope_ref,
    key_up_hbm,
    value_up_hbm,
    cache_hbm,
    length_ref,
    page_hbm,
    out_ref,
    hidden,
    weights,
    total,
    rows,
    queries,
    cache,
    value_up,
    key_up,
    pages,
    owner,
    old_best,
    old_amount,
    old_summed,
    outgoing,
    arrived,
    second,
    second_in,
    third,
    third_in,
    load_sem,
    kv_send,
    kv_recv,
    pair_send,
    pair_recv,
    q_send,
    q_recv,
    cache_send,
    cache_recv,
    rows_send,
    rows_recv,
    one_send,
    one_recv,
    two_send,
    two_recv,
    three_send,
    three_recv,
):
    x, z, y, core = place()
    depth = kv_hbm.shape[0]
    half = depth // 2
    chunk = depth * 8
    sibling = {"ctx": ctx_of(z, y, 1 - core)}

    barrier = pltpu.get_barrier_semaphore()
    pl.semaphore_signal(barrier, inc=1, device_id=sibling, device_id_type=MESH)
    for step in (1, 2, 3):
        for device in (
            {"role": (x + step) % 4},
            {"ctx": ctx_of((z + step) % 4, y, core)},
            {"ctx": ctx_of(z, (y + step) % 4, core)},
        ):
            pl.semaphore_signal(barrier, inc=1, device_id=device, device_id_type=MESH)

    line = [flip(z, turn) for turn in RING]
    own_rows = pl.ds(pl.multiple_of(ctx_of(z, y, core) * depth, 16), depth)
    own_load = pltpu.make_async_copy(kv_hbm, weights.at[own_rows, :], load_sem.at[4])
    own_load.start()
    loads = []
    for index in range(4):
        columns = pl.ds(pl.multiple_of(line[index] * chunk, 128), chunk)
        loads.append(
            pltpu.make_async_copy(
                hidden_hbm.at[:, columns], hidden.at[:, columns], load_sem.at[index]
            )
        )
    page_start = pl.multiple_of((x * 16 + z * 4 + y) * pages.shape[1], 128)
    others = [
        pltpu.make_async_copy(
            page_hbm.at[:, pl.ds(page_start, pages.shape[1])], pages, load_sem.at[5]
        ),
        pltpu.make_async_copy(cache_hbm, cache.at[core], load_sem.at[6]),
        pltpu.make_async_copy(value_up_hbm, value_up, load_sem.at[7]),
        pltpu.make_async_copy(key_up_hbm, key_up, load_sem.at[8]),
    ]

    heads = key_up.shape[0]
    row = lax.broadcasted_iota(jnp.int32, (16, 1), 0) % heads

    own_load.wait()
    pl.semaphore_wait(barrier, 10)

    def piece(z_at, y_at, core_at, part):
        start = ctx_of(z_at, y_at, core_at) * depth + part * half
        return weights.at[pl.ds(pl.multiple_of(start, 16), half), :]

    def spot(part, first, second):
        return (second, first) if part == 0 else (first, second)

    mine = [(y, z), (z, y)]
    sends = []

    def begin(copy):
        copy.start()
        sends.append(copy)

    def send(part, slot, where, target):
        ref = piece(*spot(part, *where), core, part)
        device = {"ctx": ctx_of(*spot(part, *target), core)}
        begin(remote(ref, ref, kv_send.at[part, slot], kv_recv.at[part, slot], device))

    def pair(part, slot, where, core_at):
        ref = piece(*spot(part, *where), core_at, part)
        return remote(ref, ref, pair_send.at[part, slot], pair_recv.at[part, slot], sibling)

    def places(part):
        first, second = mine[part]
        along = [flip(first, turn) for turn in RING]
        found = {15: (first, second)}
        for index in range(4):
            if index < 3:
                found[index] = (along[index + 1], second)
            found[3 + index] = (along[index], flip(second, NEAR))
            found[7 + index] = (along[index], flip(second, SIDE))
            found[11 + index] = (along[index], flip(second, FAR))
        return found

    table = [places(0), places(1)]

    def pass_on(part, slot):
        begin(pair(part, slot, table[part][slot], core))

    seen = set()

    def need(part, *slots):
        for slot in slots:
            if (part, slot) not in seen and slot != 15:
                seen.add((part, slot))
                ref = piece(*spot(part, *table[part][slot]), core, part)
                remote(
                    ref, ref, kv_send.at[part, slot], kv_recv.at[part, slot], sibling
                ).wait_recv()
                pass_on(part, slot)

    def spread(part, index):
        first, second = mine[part]
        where = table[part][(15, 0, 1, 2)[index]]
        need(part, (15, 0, 1, 2)[index])
        send(part, 3 + index, where, (first, flip(second, NEAR)))
        send(part, 7 + index, where, (first, flip(second, SIDE)))

    def opposite(part):
        first, second = mine[part]
        need(part, 0, 1)
        source = jnp.where(core == 0, flip(first, NEAR), flip(first, SIDE))
        target = jnp.where(core == 0, flip(first, SIDE), flip(first, NEAR))
        send(part, 2, (source, second), (target, second))

    def onward(part, index):
        first, second = mine[part]
        slot, turn = (3 + index, SIDE) if index < 2 else (7 + index, NEAR)
        need(part, slot)
        send(part, 11 + index, table[part][slot], (first, flip(second, turn)))

    one_at, two_at = jnp.where(core == 0, z, y), jnp.where(core == 0, y, z)

    def q_spot(first, second):
        return jnp.where(core == 0, first, second), jnp.where(core == 0, second, first)

    def q_copies(stage, step, sending):
        sign = 0 if sending else 4 - step
        if stage == 0:
            ref = queries.at[(x, *q_spot((one_at + sign) % 4, two_at), core)]
            device = {"ctx": ctx_of(*q_spot((one_at + step) % 4, two_at), core)}
            return [remote(ref, ref, q_send.at[0, step, 0], q_recv.at[0, step, 0], device)]
        if stage == 1:
            device = {"ctx": ctx_of(*q_spot(one_at, (two_at + step) % 4), core)}
            copies = []
            for index in range(4):
                ref = queries.at[
                    (x, *q_spot((one_at + index) % 4, (two_at + sign) % 4), core)
                ]
                copies.append(
                    remote(ref, ref, q_send.at[1, step, index], q_recv.at[1, step, index], device)
                )
            return copies
        ref = queries.at[(x + sign) % 4, :, :, core]
        device = {"role": (x + step) % 4}
        return [remote(ref, ref, q_send.at[2, step, 0], q_recv.at[2, step, 0], device)]

    def q_wait(stage):
        for step in (1, 3, 2):
            for copy in q_copies(stage, step, False):
                copy.wait_recv()

    def q_stage(stage):
        if stage > 0:
            q_wait(stage - 1)
        for step in (1, 3, 2):
            for copy in q_copies(stage, step, True):
                begin(copy)

    loaded = set()

    def pieces_of(index, side):
        lines = (15, 0, 1, 2)
        base = (None, 3, 7, 11)[index]
        one = [lines[k] if index == 0 else base + k for k in ((0, 1), (2, 3))[side]]
        two = ((lines[index], 3 + index), (7 + index, 11 + index))[side]
        return [(0, slot) for slot in one] + [(1, slot) for slot in two]

    def gather(index, side):
        for part, slot in pieces_of(index, side):
            need(part, slot)

    def multiply(index, side, tile):
        if tile == 0:
            gather(index, side)
            for part, slot in pieces_of(index, side):
                pair(part, slot, table[part][slot], 1 - core).wait_recv()
            if index not in loaded:
                loaded.add(index)
                loads[index].wait()
        start = line[index] * chunk + (y // 2 if side == 0 else 1 - y // 2) * (chunk // 2)
        columns = pl.ds(pl.multiple_of(start, 128), chunk // 2)
        down = pl.ds(pl.multiple_of(start, 128), chunk // 2)
        span = pl.ds(tile * 512, 512)
        product = jnp.dot(
            hidden[span, columns], weights[down, :], preferred_element_type=jnp.float32
        )
        if index == 0 and side == 0:
            total[span, :] = product
        else:
            total[span, :] += product

    def queries_of(group):
        return queries[group, :, :, core].reshape(256, 576)

    row_request = lax.broadcasted_iota(jnp.int32, (256, 1), 0) // 8 % 2

    def cache_pair(core_at):
        return remote(
            cache_hbm, cache.at[core_at], cache_send.at[0], cache_recv.at[0], sibling
        )

    def cached(turn):
        if turn == 0:
            others[1].wait()
        else:
            cache_pair(1 - core).wait_recv()
        source = core if turn == 0 else 1 - core
        slots = cache.shape[3]
        position = ctx_of(z, y, source) * slots + lax.broadcasted_iota(jnp.int32, (1, slots), 1)
        blocks = []
        for request in (0, 1):
            live = (position < length_ref[x * 2 + request]) & (row_request == request)
            blocks.append((cache[source, request], live, True))
        found = attend(queries_of(x), blocks, scale)
        if turn == 1:
            found = merge_two(found, (old_best[...], old_amount[...], old_summed[...]))
        old_best[...], old_amount[...], old_summed[...] = found

    for part in (0, 1):
        first, second_at = mine[part]
        send(part, 0, (first, second_at), (flip(first, NEAR), second_at))
        send(part, 1, (first, second_at), (flip(first, SIDE), second_at))
    for copy in (others[3], others[0], others[1], others[2]):
        copy.start()
    for load in loads:
        load.start()
    for part in (0, 1):
        pass_on(part, 15)

    nope = jnp.concatenate(
        [nope_ref[r, t].astype(jnp.float32) for r in (0, 1) for t in (0, 1)], axis=0
    ).astype(jnp.bfloat16)
    rope = jnp.concatenate(
        [rope_ref[r, t].astype(jnp.float32) for r in (0, 1) for t in (0, 1)], axis=0
    )
    others[3].wait()
    absorbed = jnp.zeros((16, LATENT), jnp.float32)
    for head in range(heads):
        product = jnp.dot(nope, key_up[head], preferred_element_type=jnp.float32)
        absorbed = jnp.where(row == head, product, absorbed)
    queries[x, z, y, core, :, :LATENT] = absorbed.astype(jnp.bfloat16)
    queries[x, z, y, core, :, LATENT:] = rope.astype(jnp.bfloat16)
    others[0].wait()
    bins = pages[...]
    request_of = (bins // 64 * 2 + bins % 2).astype(jnp.float32)
    count = pages.shape[1] // 2
    page = lax.broadcasted_iota(jnp.int32, (count, count * PAGE), 0)
    key = lax.broadcasted_iota(jnp.int32, (count, count * PAGE), 1)
    spread_out = (key // PAGE == page).astype(jnp.float32).astype(jnp.bfloat16)
    request_of = jnp.concatenate([request_of[:, :count], request_of[:, count:]], axis=0)
    wide = jnp.concatenate([request_of] * 4, axis=0).astype(jnp.bfloat16)
    owner[...] = jnp.dot(wide, spread_out, preferred_element_type=jnp.float32)[0:2, :]

    for kind, *numbers in PLAN:
        if kind == "p":
            spread(*numbers)
        elif kind == "o":
            opposite(*numbers)
        elif kind == "n":
            onward(*numbers)
        elif kind == "q":
            q_stage(*numbers)
        elif kind == "w":
            gather(*numbers)
        elif kind == "c":
            begin(cache_pair(core))
        elif kind == "k":
            cached(*numbers)
        else:
            multiply(*numbers)

    def rows_pair(tile, core_at):
        ref = rows.at[core_at, pl.ds(tile * 256, 256), :]
        return remote(ref, ref, rows_send.at[tile], rows_recv.at[tile], sibling)

    for tile in range(4):
        span = pl.ds(tile * 256, 256)
        latent = total[span, :LATENT]
        inverse = lax.rsqrt(jnp.mean(latent * latent, axis=-1, keepdims=True) + 1e-06)
        rows[core, span, :LATENT] = (latent * inverse * gain_ref[...]).astype(jnp.bfloat16)
        rows[core, span, LATENT:] = total[span, LATENT:].astype(jnp.bfloat16)
        begin(rows_pair(tile, core))

    def compute(step):
        turn = TURNS[step]
        group = (x + turn) % 4
        if turn != 0:
            for copy in q_copies(2, 4 - turn, False):
                copy.wait_recv()
        if step == 0:
            for tile in range(4):
                rows_pair(tile, 1 - core).wait_recv()
        wanted = (group * 2 + row_request).astype(jnp.float32)
        blocks = []
        for source in (core, 1 - core):
            blocks.append((rows[source], owner[pl.ds(source, 1), :] == wanted, False))
        found = attend(queries_of(group), blocks, scale)
        if turn == 0:
            found = merge_two(found, (old_best[...], old_amount[...], old_summed[...]))
        best, amount, summed = found
        some = amount > 0.0
        amount = jnp.where(some, amount, 1.0)
        mark = jnp.where(some, best + jnp.log2(amount), LOW)
        block, tail = pack(summed * (1.0 / amount), mark)
        outgoing[step, :, :, :, :LATENT] = block.reshape(4, 4, 16, LATENT)
        outgoing[step, :, :, :, LATENT:] = tail.reshape(4, 4, 16, TAIL - LATENT)

        @pl.when(core == 0)
        def _():
            for turn in (2, 1, 3):
                out_y(step, turn).start()

        @pl.when(core == 1)
        def _():
            for turn in (2, 1, 3):
                out_z(step, turn).start()

    def out_y(step, turn):
        there = (y + turn) % 4
        return remote(
            outgoing.at[step, :, there],
            arrived.at[step, turn],
            one_send.at[step, turn],
            one_recv.at[step, turn],
            {"ctx": ctx_of(z, there, core)},
        )

    def out_z(step, turn):
        there = (z + turn) % 4
        return remote(
            outgoing.at[step, there],
            arrived.at[step, turn],
            one_send.at[step, turn],
            one_recv.at[step, turn],
            {"ctx": ctx_of(there, y, core)},
        )

    def next_x(step):
        return remote(
            second.at[step],
            second_in.at[step],
            two_send.at[step],
            two_recv.at[step],
            {"role": (x + TURNS[step]) % 4},
        )

    def end_z(turn):
        there = (z + turn) % 4
        return remote(
            third.at[there],
            third_in.at[turn],
            three_send.at[turn],
            three_recv.at[turn],
            {"ctx": ctx_of(there, y, core)},
        )

    def end_y(turn):
        there = (y + turn) % 4
        return remote(
            third.at[there],
            third_in.at[turn],
            three_send.at[turn],
            three_recv.at[turn],
            {"ctx": ctx_of(z, there, core)},
        )

    def put(ref, parts):
        block, tail = pack(*joined(parts))
        ref[..., :LATENT] = block
        ref[..., LATENT:] = tail

    def merge(step):
        @pl.when(core == 0)
        def _():
            for turn in (1, 3, 2):
                out_y(step, turn).wait_recv()

        @pl.when(core == 1)
        def _():
            for turn in (1, 3, 2):
                out_z(step, turn).wait_recv()

        own = jnp.where(core == 0, outgoing[step, :, y], outgoing[step, z])
        put(second.at[step], [own] + [arrived[step, turn] for turn in (1, 2, 3)])
        if TURNS[step] != 0:
            next_x(step).start()

    for step in range(4):
        compute(step)
        if step > 0:
            merge(step - 1)
    merge(3)

    def conclude(block):
        latent = block.astype(jnp.bfloat16)
        result = jnp.zeros((16, value_up.shape[2]), jnp.float32)
        for head in range(heads):
            product = jnp.dot(latent, value_up[head], preferred_element_type=jnp.float32)
            result = jnp.where(row == head, product, result)
        for index in range(4):
            out_ref[index // 2, index % 2] = result[index * 4 : index * 4 + 4].astype(jnp.bfloat16)

    others[2].wait()
    for copy in sends:
        copy.wait_send()

    @pl.when(core == 0)
    def _():
        for turn in (1, 2, 3):
            for step in range(4):
                out_y(step, turn).wait_send()

    @pl.when(core == 1)
    def _():
        for turn in (1, 2, 3):
            for step in range(4):
                out_z(step, turn).wait_send()

    for step in range(3):
        next_x(step).wait_recv()
    put(third, [second[3]] + [second_in[step] for step in range(3)])

    @pl.when(core == 0)
    def _():
        for turn in (2, 1, 3):
            end_z(turn).start()
        for turn in (1, 3, 2):
            end_z(turn).wait_recv()

    @pl.when(core == 1)
    def _():
        for turn in (2, 1, 3):
            end_y(turn).start()
        for turn in (1, 3, 2):
            end_y(turn).wait_recv()

    own = jnp.where(core == 0, third[z], third[y])
    conclude(joined([own] + [third_in[turn] for turn in (1, 2, 3)])[0])

    for step in range(3):
        next_x(step).wait_send()

    @pl.when(core == 0)
    def _():
        for turn in (1, 2, 3):
            end_z(turn).wait_send()

    @pl.when(core == 1)
    def _():
        for turn in (1, 2, 3):
            end_y(turn).wait_send()


def local(
    prefill_hidden,
    kv_down,
    kv_gain,
    q_nope,
    q_rope,
    key_up,
    value_up,
    latent_cache,
    cache_len,
    page_list,
):
    rows, width = prefill_hidden.shape[0], kv_down.shape[1]
    scale = math.log2(math.e) / math.sqrt(q_nope.shape[3] + q_rope.shape[3])
    vmem = pl.BlockSpec(memory_space=pltpu.VMEM)
    smem = pl.BlockSpec(memory_space=pltpu.SMEM)
    hbm = pl.BlockSpec(memory_space=pl.ANY)
    bf16, f32, dma = jnp.bfloat16, jnp.float32, pltpu.SemaphoreType.DMA
    flipped = jnp.swapaxes(latent_cache, 1, 2)
    return pl.pallas_call(
        functools.partial(kernel, scale),
        out_shape=jax.ShapeDtypeStruct(q_nope.shape[:3] + (value_up.shape[2],), bf16),
        in_specs=[hbm, hbm, vmem, vmem, vmem, hbm, hbm, hbm, smem, hbm],
        out_specs=vmem,
        scratch_shapes=[
            pltpu.VMEM(prefill_hidden.shape, bf16),
            pltpu.VMEM((prefill_hidden.shape[1], width), bf16),
            pltpu.VMEM((rows, width), f32),
            pltpu.VMEM((2, rows, width), bf16),
            pltpu.VMEM((4, 4, 4, 2, 16, width), bf16),
            pltpu.VMEM((2,) + flipped.shape, bf16),
            pltpu.VMEM(value_up.shape, bf16),
            pltpu.VMEM(key_up.shape, bf16),
            pltpu.VMEM((1, 2 * rows // PAGE), jnp.int32),
            pltpu.VMEM((2, rows), f32),
            pltpu.VMEM((256, 1), f32),
            pltpu.VMEM((256, 1), f32),
            pltpu.VMEM((256, LATENT), f32),
            pltpu.VMEM((4, 4, 4, 16, TAIL), bf16),
            pltpu.VMEM((4, 4, 4, 16, TAIL), bf16),
            pltpu.VMEM((4, 4, 16, TAIL), bf16),
            pltpu.VMEM((4, 4, 16, TAIL), bf16),
            pltpu.VMEM((4, 16, TAIL), bf16),
            pltpu.VMEM((4, 16, TAIL), bf16),
            dma((9,)),
            dma((2, 15)),
            dma((2, 15)),
            dma((2, 16)),
            dma((2, 16)),
            dma((3, 4, 4)),
            dma((3, 4, 4)),
            dma((1,)),
            dma((1,)),
            dma((4,)),
            dma((4,)),
            dma((4, 4)),
            dma((4, 4)),
            dma((4,)),
            dma((4,)),
            dma((4,)),
            dma((4,)),
        ],
        compiler_params=pltpu.CompilerParams(
            collective_id=0, has_side_effects=True, vmem_limit_bytes=60 * 2**20
        ),
    )(
        prefill_hidden,
        kv_down,
        kv_gain.reshape(1, -1),
        q_nope,
        q_rope,
        key_up,
        value_up,
        flipped,
        cache_len,
        page_list.reshape(1, -1),
    )


def solution(mesh):
    return jax.shard_map(
        local,
        mesh=mesh,
        in_specs=(
            P(("role", "ctx"), None),
            P("ctx", None),
            P(),
            P("role", None, "ctx", None),
            P("role", None, "ctx", None),
            P("ctx", None, None),
            P("ctx", None, None),
            P("role", "ctx", None),
            P(),
            P(),
        ),
        out_specs=P("role", None, "ctx", None),
        check_vma=False,
    )
```
